32 devices in a mesh: groups: 2 (over x), seq: 8 (over z, y), tensor: 2 (over core).
Axes of the slice: x: 2, y: 2, z: 4, core: 2. Of those that a mesh axis runs over, the one named last changes fastest.
Arguments:
- queries: bfloat16 [128, 2, 8192], P(('groups', 'seq'), None, 'tensor'), parts along dimension 0, may hold values from -384 to 384
- fresh_keys: bfloat16 [128, 2, 1024], P(('groups', 'seq'), None, 'tensor'), parts along dimension 0, may hold values from -24 to 24
- fresh_values: bfloat16 [128, 2, 1024], P(('groups', 'seq'), None, 'tensor'), parts along dimension 0, may hold values from -6 to 6
- residual_in: bfloat16 [128, 2, 8192], P(('groups', 'seq'), None, 'tensor'), parts along dimension 0, may hold values from -0.29882812 to 0.29882812
- cache_keys: bfloat16 [8, 8192, 128], P('tensor', ('groups', 'seq')), parts along dimension 1, may hold values from -8 to 8
- cache_values: bfloat16 [8, 8192, 128], P('tensor', ('groups', 'seq')), parts along dimension 1, may hold values from -6 to 6
- key_scales: float32 [8, 128], P('tensor', ('groups', 'seq')), parts along dimension 1, may hold values from 0.5 to 2
- value_scales: float32 [8, 128], P('tensor', ('groups', 'seq')), parts along dimension 1, may hold values from 0.5 to 2
- page_table: int32 [16, 8], P(('groups', 'seq')), parts along dimension 0, may hold values from 0 to 7, each once within a row
- row_lengths: int32 [128], P('groups'), parts along dimension 0, may hold values from 512 to 4096
- norm_gain: float32 [8192], P('tensor'), may hold values from 0.1 to 1.9
- w_gate: bfloat16 [8192, 14336], P('tensor', 'seq'), may hold values from -0.0625 to 0.0625
- w_up: bfloat16 [8192, 14336], P('tensor', 'seq'), may hold values from -0.0625 to 0.0625
- w_down: bfloat16 [14336, 8192], P('seq', 'tensor'), may hold values from -0.046875 to 0.046875
Outputs:
- layer_out: bfloat16 [128, 2, 8192], P(('groups', 'seq'), None, 'tensor'), parts along dimension 0
The draws below stay inside these ranges and needn't reach their ends.
There are 2 independent parts, one for each index of `groups`. The reference program is written for one: setup_inputs(seed, part) draws one part's arguments, and reference() takes and returns one part's arrays. A program takes and returns all parts, laid end to end along the dimension named above; an argument that names none is the same for every part. Nothing has to cross between parts.
Inputs may be any that keep to these rules, and one draw needn't show every extreme that they name: Each row of page_table names each of its seq index's pages once. `row_lengths`: every row sees at least the cache positions of the first seq index.
All inputs are finite; a program needn't handle non-finite values.
Results may differ from the reference program's by a relative error of at most 0.0064.
Values may be sent and summed in bfloat16 or wider, within the bound.
A program may use at most 128 MiB of HBM per device.

```python
import math
import jax
import jax.numpy as jnp
from jax import lax

D = 8192
H = 64
KVH = 8
HD = 128
FF = 14336
ROWS = 64
STEPS = 2
BLK = 64
CACHE_DEV = 512
CACHE = 4096
BPD = 8
N_SEQ = 8


def drawn_pair(key):
    base_key = jax.random.fold_in(key, 11)
    key_draw = jax.random.fold_in(base_key, 1)
    query_draw = jax.random.fold_in(base_key, 2)
    cache_rows = jnp.clip(jax.random.normal(key_draw, (KVH, CACHE, HD), jnp.float32), -6.0, 6.0)
    query_rows = jnp.clip(2.0 * jax.random.normal(query_draw, (ROWS, STEPS, D), jnp.float32), -12.0, 12.0)
    return (cache_rows, query_rows)


def draw_cache_keys(key, part):
    return drawn_pair(key)[0].astype(jnp.bfloat16)


def draw_queries(key, part):
    return drawn_pair(key)[1].astype(jnp.bfloat16)


def place_ends(result, rng, least, high):
    extent = result.shape
    index_at = [jax.random.randint(jax.random.fold_in(rng, axis), (), 0, extent[axis]) for axis in range(len(extent))]
    result = result.at[tuple(index_at)].set(least)
    longest = extent.index(max(extent))
    index_at[longest] = (index_at[longest] + 1) % extent[longest]
    return result.at[tuple(index_at)].set(high)


def levels(key, extent, pieces, least, high):
    def one(axis_at, parts):
        draws = jax.random.uniform(jax.random.fold_in(jax.random.fold_in(key, 6), axis_at), (parts,), jnp.float32, least / len(pieces), high / len(pieces))
        return jnp.repeat(jnp.exp(draws), extent[axis_at] // parts).reshape((-1,) + (1,) * (len(extent) - axis_at - 1))

    loudness = one(*pieces[0])
    for cut in pieces[1:]:
        loudness = loudness * one(*cut)
    return loudness


def bell_draw(stream_key, dims, spread, bound, shards=(), kind=jnp.bfloat16):
    values = spread * jax.random.normal(stream_key, dims, jnp.float32)
    if shards:
        values = values * levels(stream_key, dims, shards, -0.22, 0.18)
    return jnp.clip(values, -bound, bound).astype(kind)


def setup_inputs(seed: int = 0, part: int = 0) -> dict:
    seeds = jax.random.split(jax.random.key(seed), 15)
    own_keys = jax.random.split(jax.random.fold_in(seeds[14], part), 15)
    return {
        "queries": draw_queries(jax.random.fold_in(jax.random.fold_in(seeds[14], part), 71), part),
        "fresh_keys": bell_draw(own_keys[1], (ROWS, STEPS, KVH * HD), 4.0, 24.0, ((0, 8), (2, 2))),
        "fresh_values": bell_draw(own_keys[2], (ROWS, STEPS, KVH * HD), 1.0, 6.0, ((0, 8), (2, 2))),
        "residual_in": bell_draw(own_keys[3], (ROWS, STEPS, D), 0.05, 0.29882812, ((0, 8), (2, 2))),
        "cache_keys": draw_cache_keys(jax.random.fold_in(jax.random.fold_in(seeds[14], part), 71), part),
        "cache_values": bell_draw(own_keys[5], (KVH, CACHE, HD), 1.0, 6.0, ((0, 2), (1, 8))),
        "key_scales": jnp.clip(jnp.exp(math.log(2.0) - 1.3862944 * jax.random.uniform(own_keys[6], (KVH, CACHE // BLK), jnp.float32) ** levels(own_keys[6], (KVH, CACHE // BLK), ((0, 2), (1, 8)), -0.2, 0.2)), 0.5, 2.0),
        "value_scales": jnp.clip(jnp.exp(math.log(2.0) - 1.3862944 * jax.random.uniform(own_keys[7], (KVH, CACHE // BLK), jnp.float32) ** levels(own_keys[7], (KVH, CACHE // BLK), ((0, 2), (1, 8)), -0.2, 0.2)), 0.5, 2.0),
        "page_table": jax.vmap(lambda own: jax.random.permutation(own, BPD))(jax.random.split(own_keys[8], N_SEQ)).reshape((N_SEQ, BPD)).astype(jnp.int32),
        "row_lengths": place_ends(jax.random.randint(own_keys[9], (ROWS,), CACHE_DEV, CACHE + 1), jax.random.fold_in(own_keys[9], 1), CACHE_DEV, CACHE).astype(jnp.int32),
        "norm_gain": jnp.clip(1.0 + 0.18 * jax.random.normal(seeds[10], (D,), jnp.float32), 0.1, 1.9),
        "w_gate": bell_draw(seeds[11], (D, FF), D ** -0.5, 0.0625, ((0, 2), (1, 8))),
        "w_up": bell_draw(seeds[12], (D, FF), D ** -0.5, 0.0625, ((0, 2), (1, 8))),
        "w_down": bell_draw(seeds[13], (FF, D), FF ** -0.5, 0.046875, ((0, 8), (1, 2))),
    }


NEG_FILL = -1e+30
EPSILON = 1e-05
LOG2E = 1.4426950408889634

def reference(queries, fresh_keys, fresh_values, residual_in, cache_keys, cache_values, key_scales, value_scales, page_table, row_lengths, norm_gain, w_gate, w_up, w_down):
    heads_per = H // KVH
    inv_root = LOG2E / math.sqrt(HD)
    cache_index = jnp.arange(CACHE, dtype=jnp.int32)
    device_of = (cache_index // CACHE_DEV).astype(jnp.int32)
    slot_block = (cache_index % CACHE_DEV // BLK).astype(jnp.int32)
    logical = device_of * BPD + page_table[device_of, slot_block].astype(jnp.int32)
    position = logical * BLK + cache_index % BLK
    visible = position[None, :] < row_lengths[:, None]
    k_scale = jnp.repeat(key_scales, BLK, axis=1)
    v_scale = jnp.repeat(value_scales, BLK, axis=1)
    fresh_k = jnp.moveaxis(fresh_keys.reshape(ROWS, STEPS, KVH, HD), 2, 0).astype(jnp.float32)
    fresh_v = jnp.moveaxis(fresh_values.reshape(ROWS, STEPS, KVH, HD), 2, 0).astype(jnp.float32)
    results = []
    for step_index in range(STEPS):
        q_step = jnp.moveaxis(queries[:, step_index].reshape(ROWS, KVH, heads_per, HD), 1, 0).astype(jnp.float32)
        allowed = jnp.arange(STEPS) <= step_index

        def per_group(operands):
            q_group, key_block, value_block, k_row, v_row, fk_group, fv_group = operands
            raw_scores = jnp.einsum('rqd,cd->rqc', q_group, key_block.astype(jnp.float32), precision=lax.Precision.HIGHEST)
            scores = raw_scores * k_row * inv_root
            fresh_scores = jnp.einsum('rqd,rtd->rqt', q_group, fk_group, precision=lax.Precision.HIGHEST) * inv_root
            cache_mask = visible[:, None, :]
            fresh_mask = allowed[None, None, :]
            row_top = jnp.maximum(lax.optimization_barrier(jnp.max(jnp.where(cache_mask, scores, NEG_FILL), axis=-1)), lax.optimization_barrier(jnp.max(jnp.where(fresh_mask, fresh_scores, NEG_FILL), axis=-1)))
            row_top = jnp.ceil(row_top)
            cache_terms = jnp.where(cache_mask, jnp.exp2(scores - row_top[..., None]), 0.0)
            fresh_terms = jnp.where(fresh_mask, jnp.exp2(fresh_scores - row_top[..., None]), 0.0)
            row_total = lax.optimization_barrier(jnp.sum(cache_terms, axis=-1)) + lax.optimization_barrier(jnp.sum(fresh_terms, axis=-1))
            cache_weights = lax.optimization_barrier((cache_terms * v_row).astype(jnp.bfloat16)).astype(jnp.float32)
            fresh_weights = lax.optimization_barrier(fresh_terms.astype(jnp.bfloat16)).astype(jnp.float32)
            weighted = jnp.einsum('rqc,cd->rqd', cache_weights, value_block.astype(jnp.float32), precision=lax.Precision.HIGHEST)
            weighted = weighted + jnp.einsum('rqt,rtd->rqd', fresh_weights, fv_group, precision=lax.Precision.HIGHEST)
            return weighted / row_total[..., None]
        attention = lax.map(per_group, (q_step, cache_keys, cache_values, k_scale, v_scale, fresh_k, fresh_v))
        attention = jnp.moveaxis(attention, 0, 1).reshape(ROWS, D)
        hidden_state = residual_in[:, step_index].astype(jnp.float32) + attention
        inverse_rms = lax.rsqrt(lax.optimization_barrier(jnp.sum(hidden_state * hidden_state, axis=-1)) / D + EPSILON)
        normed = (hidden_state * inverse_rms[:, None] * norm_gain).astype(jnp.bfloat16)
        gate_sums = jnp.dot(normed, w_gate, preferred_element_type=jnp.float32)
        up_sums = jnp.dot(normed, w_up, preferred_element_type=jnp.float32)
        hidden = (jax.nn.silu(gate_sums) * up_sums).astype(jnp.bfloat16)
        down_sums = jnp.dot(hidden, w_down, preferred_element_type=jnp.float32)
        results.append((hidden_state + down_sums).astype(jnp.bfloat16))
    return jnp.stack(results, axis=1)
```

```python
import functools
import math

import jax
import jax.numpy as jnp
from jax import lax
from jax.experimental import pallas as pl
from jax.experimental.pallas import tpu as pltpu
from jax.sharding import PartitionSpec as P

D = 8192


NEG_FILL = -1e30
EPSILON = 1e-05
LOG2E = 1.4426950408889634


def combine_partials(earlier, later):
    shared_top = jnp.maximum(earlier[0], later[0])
    early_factor = jnp.exp2(earlier[0] - shared_top)
    late_factor = jnp.exp2(later[0] - shared_top)
    return (
        shared_top,
        earlier[1] * early_factor + later[1] * late_factor,
        earlier[2] * early_factor[..., None] + later[2] * late_factor[..., None],
    )


def masked_terms(scores, allowed_mask):
    row_top = jnp.ceil(jnp.max(jnp.where(allowed_mask, scores, NEG_FILL), axis=-1))
    exp_terms = jnp.where(allowed_mask, jnp.exp2(scores - row_top[..., None]), 0.0)
    return (row_top, exp_terms)


def plain_body(
    queries,
    fresh_keys,
    fresh_values,
    residual_in,
    cache_keys,
    cache_values,
    key_scales,
    value_scales,
    page_table,
    row_lengths,
    norm_gain,
    w_gate,
    w_up,
    w_down,
):
    local_rows = queries.shape[0]
    step_count = queries.shape[1]
    half_width = queries.shape[2]
    groups = cache_keys.shape[0]
    cache_span = cache_keys.shape[1]
    head_dim = cache_keys.shape[2]
    page_count = page_table.shape[1]
    block_size = cache_span // page_count
    heads_per = half_width // (groups * head_dim)
    inv_root = LOG2E / math.sqrt(head_dim)
    seq_index = lax.axis_index("seq")
    all_q, all_fk, all_fv, all_x = (
        lax.all_gather(queries, "seq", axis=0, tiled=True),
        lax.all_gather(fresh_keys, "seq", axis=0, tiled=True),
        lax.all_gather(fresh_values, "seq", axis=0, tiled=True),
        lax.all_gather(residual_in, "seq", axis=0, tiled=True),
    )
    all_rows = all_q.shape[0]
    offsets = jnp.arange(cache_span, dtype=jnp.int32)
    logical = seq_index * page_count + jnp.repeat(page_table[0], block_size)
    position = logical * block_size + offsets % block_size
    visible = position[None, :] < row_lengths[:, None]
    k_scale = jnp.repeat(key_scales, block_size, axis=1)
    v_scale = jnp.repeat(value_scales, block_size, axis=1)
    q_part = all_q.reshape(all_rows, step_count, groups, heads_per, head_dim)
    q_part = jnp.moveaxis(q_part, 2, 0)

    def per_group(operands):
        q_group, key_block, value_block, k_row, v_row = operands
        raw_scores = jnp.einsum(
            "nsqd,cd->nsqc", q_group, key_block, preferred_element_type=jnp.float32
        )
        scores = raw_scores * k_row * inv_root
        row_top, exp_terms = masked_terms(scores, visible[:, None, None, :])
        row_total = jnp.sum(exp_terms, axis=-1)
        weights = (exp_terms * v_row).astype(jnp.bfloat16)
        weighted = jnp.einsum(
            "nsqc,cd->nsqd", weights, value_block, preferred_element_type=jnp.float32
        )
        return (row_top, row_total, weighted)

    partial_value = lax.map(per_group, (q_part, cache_keys, cache_values, k_scale, v_scale))
    row_peak = lax.pmax(partial_value[0], "seq")
    factor = jnp.exp2(partial_value[0] - row_peak)
    row_total, weighted = lax.psum(
        (partial_value[1] * factor, partial_value[2] * factor[..., None]), "seq"
    )
    row_count = all_q.shape[0]
    fresh_row_count = all_q.shape[0]
    q_part = all_q.reshape(fresh_row_count, step_count, groups, heads_per, head_dim)
    k_part = all_fk.reshape(fresh_row_count, step_count, groups, head_dim)
    v_part = all_fv.reshape(fresh_row_count, step_count, groups, head_dim)
    raw_scores = jnp.einsum("nsgqd,ntgd->gnsqt", q_part, k_part, preferred_element_type=jnp.float32)
    scores = raw_scores * inv_root
    allowed = jnp.arange(step_count)[None, :] <= (0 + jnp.arange(step_count))[:, None]
    row_top, exp_terms = masked_terms(scores, allowed[None, None, :, None, :])
    fresh_row_total = jnp.sum(exp_terms, axis=-1)
    fresh_weighted = jnp.einsum(
        "gnsqt,ntgd->gnsqd",
        exp_terms.astype(jnp.bfloat16),
        v_part,
        preferred_element_type=jnp.float32,
    )
    joined = combine_partials(
        (row_peak, row_total, weighted), (row_top, fresh_row_total, fresh_weighted)
    )
    attention = joined[2] / joined[1][..., None]
    attention = jnp.moveaxis(attention, 0, 2).reshape(row_count, step_count, half_width)
    hidden_state = all_x.astype(jnp.float32) + attention
    square = lax.psum(jnp.sum(hidden_state * hidden_state, axis=-1), "tensor")
    inverse_rms = lax.rsqrt(square / D + EPSILON)
    normed = (hidden_state * inverse_rms[..., None] * norm_gain).astype(jnp.bfloat16)
    hidden_state, normed = (hidden_state, normed)
    own_state = lax.dynamic_slice_in_dim(hidden_state, seq_index * local_rows, local_rows, 0)
    flat_normed = normed.reshape(all_rows * step_count, half_width)
    gate_part = jnp.dot(flat_normed, w_gate, preferred_element_type=jnp.float32)
    up_part = jnp.dot(flat_normed, w_up, preferred_element_type=jnp.float32)
    gate_sums, up_sums = lax.psum((gate_part, up_part), "tensor")
    hidden = (jax.nn.silu(gate_sums) * up_sums).astype(jnp.bfloat16)
    down_sums = lax.psum_scatter(
        jnp.dot(hidden, w_down, preferred_element_type=jnp.float32),
        "seq",
        scatter_dimension=0,
        tiled=True,
    )
    return (own_state + down_sums.reshape(local_rows, step_count, half_width)).astype(jnp.bfloat16)


MESH = pl.DeviceIdType.MESH
FLOOR = -1e29
CHUNKS = 4
W_PIECES = 4
TILE = 256


def layer_kernel(
    lines,
    steps,
    q_ref,
    fk_ref,
    fv_ref,
    res_ref,
    lens_ref,
    ks_ref,
    vs_ref,
    pt_ref,
    gain_ref,
    ck_hbm,
    cv_hbm,
    wg_hbm,
    wu_hbm,
    wd_hbm,
    out_ref,
    kbuf,
    vbuf,
    wgu,
    wd,
    qbuf,
    krow,
    vrow,
    prow,
    fkp,
    fvp,
    facc,
    fstat,
    part,
    stat,
    ypart,
    ystat,
    spart,
    sstat,
    zpart,
    zstat,
    hs,
    sq,
    nbuf,
    gsend,
    grecv,
    gown,
    hbuf,
    dacc,
    dpart,
    dy,
    dsum,
    dz,
    local_sem,
    w_sem,
    qz_sem,
    qy_sem,
    py_sem,
    pz_sem,
    sq_sem,
    nz_sem,
    ny_sem,
    g_sem,
    h_sem,
    dy_sem,
    dz_sem,
):
    f32 = jnp.float32
    bf16 = jnp.bfloat16
    seq = lax.axis_index("seq")
    core = lax.axis_index("tensor")
    z, y = seq // 2, lax.rem(seq, 2)
    groups, span, hd = kbuf.shape
    rows, width = q_ref.shape
    heads = width // hd
    per = heads // groups
    pages = pt_ref.shape[1]
    page = span // pages
    inv_root = LOG2E / math.sqrt(hd)

    def line(d):
        return lax.rem(z + d, lines)

    def to_y():
        return {"seq": z * 2 + 1 - y}

    def to_z(zz):
        return {"seq": zz * 2 + y}

    def to_core():
        return {"tensor": 1 - core}

    def remote(src, dst, sems, send_at, recv_at, where):
        return pltpu.make_async_remote_copy(
            src_ref=src,
            dst_ref=dst,
            send_sem=sems.at[0, send_at],
            recv_sem=sems.at[1, recv_at],
            device_id=where,
            device_id_type=MESH,
        )

    cache_copies = [
        pltpu.make_async_copy(ck_hbm, kbuf, local_sem.at[0]),
        pltpu.make_async_copy(cv_hbm, vbuf, local_sem.at[1]),
    ]
    half = hbuf.shape[2]
    weight_copies = []
    for i, src in enumerate((wg_hbm, wu_hbm)):
        for h in range(2):
            piece = src.shape[0] // W_PIECES
            for k in range(W_PIECES):
                at = pl.ds(k * piece, piece)
                weight_copies.append(
                    pltpu.make_async_copy(
                        src.at[at, pl.ds(h * half, half)],
                        wgu.at[h, at, pl.ds(i * half, half)],
                        w_sem.at[2 * i + h, k],
                    )
                )
    down_copies = []
    for k in range(W_PIECES):
        piece = wd_hbm.shape[0] // W_PIECES
        at = pl.ds(k * piece, piece)
        down_copies.append(pltpu.make_async_copy(wd_hbm.at[at], wd.at[at], w_sem.at[4, k]))
    for copy in cache_copies:
        copy.start()

    qbuf[y, z] = q_ref[...]

    barrier = pltpu.get_barrier_semaphore()
    peers = [to_y(), to_core()] + [to_z(line(d)) for d in range(1, lines)]
    for where in peers:
        pl.semaphore_signal(barrier, inc=1, device_id=where, device_id_type=MESH)
    pl.semaphore_wait(barrier, len(peers))

    def gather_z(buf, sems, d):
        return remote(buf.at[y, z], buf.at[y, z], sems, d, z, to_z(line(d)))

    def gather_z_arrival(buf, sems, zz):
        return remote(buf.at[y, zz], buf.at[y, zz], sems, 0, zz, to_z(zz))

    def gather_y(buf, sems, zz):
        return remote(buf.at[y, zz], buf.at[y, zz], sems, zz, zz, to_y())

    def gather_y_arrival(buf, sems, zz):
        return remote(buf.at[1 - y, zz], buf.at[1 - y, zz], sems, zz, zz, to_y())

    gather_y(qbuf, qy_sem, z).start()
    for d in range(1, lines):
        gather_z(qbuf, qz_sem, d).start()
    for copy in weight_copies + down_copies:
        copy.start()

    owner = lax.broadcasted_iota(jnp.int32, (1, span), 1) // page
    within = lax.rem(lax.broadcasted_iota(jnp.int32, (1, span), 1), page)
    place = jnp.zeros((1, span), jnp.int32)
    for j in range(pages):
        place = jnp.where(owner == j, pt_ref[:, j : j + 1], place)
    prow[...] = (seq * pages + place) * page + within
    for g in range(groups):
        k_line = jnp.zeros((1, span), f32)
        v_line = jnp.zeros((1, span), f32)
        for j in range(pages):
            k_line = jnp.where(owner == j, ks_ref[g : g + 1, j : j + 1], k_line)
            v_line = jnp.where(owner == j, vs_ref[g : g + 1, j : j + 1], v_line)
        krow[g] = k_line * inv_root
        vrow[g] = v_line

    lane = lax.broadcasted_iota(jnp.int32, (rows, 128), 1)

    def stacked(block, g):
        return jnp.concatenate(
            [block[:, (g * per + j) * hd : (g * per + j + 1) * hd] for j in range(per)], axis=0
        )

    def softmax_terms(scores):
        top = jnp.maximum(jnp.ceil(jnp.max(scores, axis=-1, keepdims=True)), FLOOR)
        terms = jnp.exp2(scores - top)
        return top, terms, jnp.sum(terms, axis=-1, keepdims=True)

    def spread(tops, totals, g, top, total):
        for j in range(per):
            at = slice(j * rows, (j + 1) * rows)
            tops = jnp.where(lane == g * per + j, top[at], tops)
            totals = jnp.where(lane == g * per + j, total[at], totals)
        return tops, totals

    fkp[...] = jnp.zeros_like(fkp)
    fvp[...] = jnp.zeros_like(fvp)
    fkp[0:rows] = fk_ref[...]
    fvp[0:rows] = fv_ref[...]
    slots = fkp.shape[0]
    token = lax.rem(lax.broadcasted_iota(jnp.int32, (per * rows, slots), 0), rows)
    key_token = lax.broadcasted_iota(jnp.int32, (per * rows, slots), 1)
    allowed = (token // steps == key_token // steps) & (key_token <= token)
    tops, totals = jnp.zeros((rows, 128), f32), jnp.ones((rows, 128), f32)
    for g in range(groups):
        scores = lax.dot_general(
            stacked(q_ref, g),
            fkp[:, g * hd : (g + 1) * hd],
            (((1,), (1,)), ((), ())),
            preferred_element_type=f32,
        )
        top, terms, total = softmax_terms(jnp.where(allowed, scores * inv_root, NEG_FILL))
        acc = jnp.dot(
            terms.astype(bf16), fvp[:, g * hd : (g + 1) * hd], preferred_element_type=f32
        )
        for j in range(per):
            facc[:, (g * per + j) * hd : (g * per + j + 1) * hd] = acc[j * rows : (j + 1) * rows]
        tops, totals = spread(tops, totals, g, top, total)
    fstat[0] = tops
    fstat[1] = totals

    for copy in cache_copies:
        copy.wait()

    def attend(yy, zz):
        lens = jnp.concatenate([lens_ref[yy, zz]] * per, axis=0)
        block = qbuf.at[yy, zz]
        out = part.at[yy, zz]
        tops, totals = jnp.zeros((rows, 128), f32), jnp.ones((rows, 128), f32)
        for g in range(groups):
            scores = lax.dot_general(
                stacked(block, g), kbuf[g], (((1,), (1,)), ((), ())), preferred_element_type=f32
            )
            scores = jnp.where(prow[...] < lens, scores * krow[g], NEG_FILL)
            top, terms, total = softmax_terms(scores)
            acc = jnp.dot(
                (terms * vrow[g]).astype(bf16), vbuf[g], preferred_element_type=f32
            ).astype(bf16)
            for j in range(per):
                out[:, (g * per + j) * hd : (g * per + j + 1) * hd] = acc[j * rows : (j + 1) * rows]
            tops, totals = spread(tops, totals, g, top, total)
        stat[yy, zz, 0] = tops
        stat[yy, zz, 1] = totals

    def part_y(zz):
        src = (part.at[1 - y, zz], stat.at[1 - y, zz])
        dst = (ypart.at[zz], ystat.at[zz])
        return [remote(src[i], dst[i], py_sem, i * lines + zz, i * lines + zz, to_y()) for i in range(2)]

    def part_z(zz, at):
        src, dst = (spart.at[zz], sstat.at[zz]), (zpart.at[at], zstat.at[at])
        return [
            remote(src[i], dst[i], pz_sem, i * lines + zz, i * lines + at, to_z(zz)) for i in range(2)
        ]

    def join(zz):
        for copy in part_y(zz):
            copy.wait_recv()
        first, second = stat[y, zz, 0], ystat[zz, 0]
        top = jnp.maximum(first, second)
        a, b = jnp.exp2(first - top), jnp.exp2(second - top)
        sstat[zz, 0] = top
        sstat[zz, 1] = stat[y, zz, 1] * a + ystat[zz, 1] * b
        for h in range(heads):
            at = slice(h * hd, (h + 1) * hd)
            spart[zz, :, at] = (
                part[y, zz, :, at].astype(f32) * a[:, h : h + 1]
                + ypart[zz, :, at].astype(f32) * b[:, h : h + 1]
            ).astype(bf16)
        for copy in part_z(zz, z):
            copy.start()

    @pl.loop(0, 2 * lines)
    def _(k):
        d, other = k // 2, lax.rem(k, 2)
        zz = line(d)

        @pl.when((other == 0) & (d > 0))
        def _():
            gather_z_arrival(qbuf, qz_sem, zz).wait_recv()
            gather_y(qbuf, qy_sem, zz).start()

        @pl.when(other == 1)
        def _():
            gather_y_arrival(qbuf, qy_sem, zz).wait_recv()

        attend(lax.rem(y + other, 2), zz)

        @pl.when(other == 1)
        def _():
            for copy in part_y(zz):
                copy.start()

        @pl.when((other == 1) & (d > 1))
        def _():
            join(line(d - 1))

    join(line(lines - 1))
    for copy in part_y(z):
        copy.wait_recv()

    for d in range(1, lines):
        for copy in part_z(line(d), line(d)):
            copy.wait_recv()
    stats = [fstat, stat.at[y, z], ystat.at[z]] + [zstat.at[line(d)] for d in range(1, lines)]
    parts = [facc, part.at[y, z], ypart.at[z]] + [zpart.at[line(d)] for d in range(1, lines)]
    top = functools.reduce(jnp.maximum, [s[0] for s in stats])
    factors = [jnp.exp2(s[0] - top) for s in stats]
    total = sum(s[1] * f for s, f in zip(stats, factors))
    factors = [f / total for f in factors]
    square = jnp.zeros((rows, hd), f32)
    for h in range(heads):
        at = slice(h * hd, (h + 1) * hd)
        state = res_ref[:, at].astype(f32) + sum(
            p[:, at].astype(f32) * f[:, h : h + 1] for p, f in zip(parts, factors)
        )
        hs[:, at] = state
        square += state * state
    sq[0] = jnp.broadcast_to(jnp.sum(square, axis=-1, keepdims=True), (rows, 128))
    square_copy = remote(sq.at[0], sq.at[1], sq_sem, 0, 0, to_core())
    square_copy.start()
    square_copy.wait_recv()
    inverse = lax.rsqrt((sq[0] + sq[1])[:, 0:1] / (2 * width) + EPSILON)
    nbuf[y, z] = (hs[...] * inverse * gain_ref[...]).astype(bf16)

    gather_y(nbuf, ny_sem, z).start()
    for d in range(1, lines):
        gather_z(nbuf, nz_sem, d).start()
    for d in range(1, lines):
        gather_z_arrival(nbuf, nz_sem, line(d)).wait_recv()
        gather_y(nbuf, ny_sem, line(d)).start()
    for copy in weight_copies:
        copy.wait()
    for d in range(lines):
        gather_y_arrival(nbuf, ny_sem, line(d)).wait_recv()

    all_rows = 2 * lines * rows

    def gate_up(at, out):
        @pl.loop(0, 2 * half // TILE)
        def _(t):
            columns = pl.ds(pl.multiple_of(t * TILE, TILE), TILE)
            out[:, columns] = jnp.dot(
                nbuf[...].reshape(all_rows, width),
                wgu[at, :, columns],
                preferred_element_type=f32,
            ).astype(out.dtype)

    exchange = remote(gsend, grecv, g_sem, 0, 0, to_core())
    gate_up(1 - core, gsend)
    exchange.start()
    gate_up(core, gown)
    exchange.wait_recv()
    gate = gown[:, :half] + grecv[:, :half].astype(f32)
    up = gown[:, half:] + grecv[:, half:].astype(f32)
    hbuf[core] = (gate / (1.0 + jnp.exp(-gate)) * up).astype(bf16)
    hidden_copy = remote(hbuf.at[core], hbuf.at[core], h_sem, 0, 0, to_core())
    hidden_copy.start()

    chunk = width // CHUNKS
    for copy in down_copies:
        copy.wait()

    def down(at, c, add):
        @pl.loop(0, chunk // TILE)
        def _(t):
            columns = pl.ds(pl.multiple_of(t * TILE, TILE), TILE)
            value = jnp.dot(
                hbuf[at],
                wd[
                    pl.ds(pl.multiple_of(at * half, 128), half),
                    pl.ds(pl.multiple_of(c * chunk + t * TILE, TILE), TILE),
                ],
                preferred_element_type=f32,
            ).reshape(2, lines, rows, TILE)
            if add:
                value += dacc[c, :, :, :, columns]
            dacc[c, :, :, :, columns] = value

    for c in range(CHUNKS):
        down(core, c, False)
    remote(hbuf.at[1 - core], hbuf.at[1 - core], h_sem, 0, 0, to_core()).wait_recv()

    def down_y(c):
        return remote(dpart.at[c], dy.at[c], dy_sem, c, c, to_y())

    def down_z(c, zz, at):
        return remote(
            dsum.at[c, zz], dz.at[c, at], dz_sem, c * lines + zz, c * lines + at, to_z(zz)
        )

    def relay(c):
        down_y(c).wait_recv()
        for d in range(1, lines):
            zz = line(d)
            dsum[c, zz] = (dacc[c, y, zz] + dy[c, zz].astype(f32)).astype(bf16)
            down_z(c, zz, z).start()

    for c in range(CHUNKS):
        down(1 - core, c, True)
        dpart[c] = dacc[c, 1 - y].astype(bf16)
        down_y(c).start()
        if c > 0:
            relay(c - 1)
    relay(CHUNKS - 1)
    for c in range(CHUNKS):
        at = slice(c * chunk, (c + 1) * chunk)
        value = hs[:, at] + dacc[c, y, z] + dy[c, z].astype(f32)
        for d in range(1, lines):
            down_z(c, line(d), line(d)).wait_recv()
            value += dz[c, line(d)].astype(f32)
        out_ref[:, at] = value.astype(out_ref.dtype)

    for d in range(1, lines):
        gather_z(qbuf, qz_sem, d).wait_send()
        gather_z(nbuf, nz_sem, d).wait_send()
        for copy in part_z(line(d), z):
            copy.wait_send()
        for c in range(CHUNKS):
            down_z(c, line(d), z).wait_send()
    for d in range(lines):
        gather_y(qbuf, qy_sem, line(d)).wait_send()
        gather_y(nbuf, ny_sem, line(d)).wait_send()
        for copy in part_y(line(d)):
            copy.wait_send()
    for c in range(CHUNKS):
        down_y(c).wait_send()
    square_copy.wait_send()
    hidden_copy.wait_send()
    exchange.wait_send()


def kernel_body(
    lines,
    queries,
    fresh_keys,
    fresh_values,
    residual_in,
    cache_keys,
    cache_values,
    key_scales,
    value_scales,
    page_table,
    row_lengths,
    norm_gain,
    w_gate,
    w_up,
    w_down,
):
    local_rows, steps, width = queries.shape
    groups, span, hd = cache_keys.shape
    rows = local_rows * steps
    fresh_width = fresh_keys.shape[2]
    half = w_gate.shape[1] // 2
    chunk = width // CHUNKS
    all_rows = 2 * lines * rows
    lens = row_lengths.reshape(lines, 2, local_rows, 1).transpose(1, 0, 2, 3)
    lens = jnp.broadcast_to(lens, (2, lines, local_rows, steps)).reshape(2, lines, rows, 1)
    bf16, f32 = jnp.bfloat16, jnp.float32
    vmem = pl.BlockSpec(memory_space=pltpu.VMEM)
    anywhere = pl.BlockSpec(memory_space=pl.ANY)
    dma = pltpu.SemaphoreType.DMA
    out = pl.pallas_call(
        functools.partial(layer_kernel, lines, steps),
        out_shape=jax.ShapeDtypeStruct((rows, width), bf16),
        in_specs=[vmem] * 9 + [anywhere] * 5,
        out_specs=vmem,
        scratch_shapes=[
            pltpu.VMEM((groups, span, hd), bf16),
            pltpu.VMEM((groups, span, hd), bf16),
            pltpu.VMEM((2, width, 2 * half), bf16),
            pltpu.VMEM(w_down.shape, bf16),
            pltpu.VMEM((2, lines, rows, width), bf16),
            pltpu.VMEM((groups, 1, span), f32),
            pltpu.VMEM((groups, 1, span), f32),
            pltpu.VMEM((1, span), jnp.int32),
            pltpu.VMEM((128, fresh_width), bf16),
            pltpu.VMEM((128, fresh_width), bf16),
            pltpu.VMEM((rows, width), f32),
            pltpu.VMEM((2, rows, 128), f32),
            pltpu.VMEM((2, lines, rows, width), bf16),
            pltpu.VMEM((2, lines, 2, rows, 128), f32),
            pltpu.VMEM((lines, rows, width), bf16),
            pltpu.VMEM((lines, 2, rows, 128), f32),
            pltpu.VMEM((lines, rows, width), bf16),
            pltpu.VMEM((lines, 2, rows, 128), f32),
            pltpu.VMEM((lines, rows, width), bf16),
            pltpu.VMEM((lines, 2, rows, 128), f32),
            pltpu.VMEM((rows, width), f32),
            pltpu.VMEM((2, rows, 128), f32),
            pltpu.VMEM((2, lines, rows, width), bf16),
            pltpu.VMEM((all_rows, 2 * half), bf16),
            pltpu.VMEM((all_rows, 2 * half), bf16),
            pltpu.VMEM((all_rows, 2 * half), f32),
            pltpu.VMEM((2, all_rows, half), bf16),
            pltpu.VMEM((CHUNKS, 2, lines, rows, chunk), f32),
            pltpu.VMEM((CHUNKS, lines, rows, chunk), bf16),
            pltpu.VMEM((CHUNKS, lines, rows, chunk), bf16),
            pltpu.VMEM((CHUNKS, lines, rows, chunk), bf16),
            pltpu.VMEM((CHUNKS, lines, rows, chunk), bf16),
            dma((2,)),
            dma((5, W_PIECES)),
            dma((2, lines)),
            dma((2, lines)),
            dma((2, 2 * lines)),
            dma((2, 2 * lines)),
            dma((2, 1)),
            dma((2, lines)),
            dma((2, lines)),
            dma((2, 1)),
            dma((2, 1)),
            dma((2, CHUNKS)),
            dma((2, CHUNKS * lines)),
        ],
        compiler_params=pltpu.CompilerParams(
            collective_id=0, has_side_effects=True, vmem_limit_bytes=60 * 1024 * 1024
        ),
    )(
        queries.reshape(rows, width),
        fresh_keys.reshape(rows, fresh_width),
        fresh_values.reshape(rows, fresh_width),
        residual_in.reshape(rows, width),
        lens,
        key_scales,
        value_scales,
        page_table,
        norm_gain.reshape(1, width),
        cache_keys,
        cache_values,
        w_gate,
        w_up,
        w_down,
    )
    return out.reshape(local_rows, steps, width)


def choose_body(seq_size, cores, *args):
    local_rows, steps, width = args[0].shape
    head_dim = args[4].shape[2]
    rows, hidden = local_rows * steps, args[11].shape[1]
    heads = width // head_dim
    weights = 2 * 3 * width * hidden
    fits = (
        cores == 2
        and seq_size % 2 == 0
        and rows % 16 == 0
        and rows <= 128
        and hidden % 256 == 0
        and width % (CHUNKS * TILE) == 0
        and head_dim == 128
        and heads <= 128
        and weights <= 44 * 1024 * 1024
    )
    if fits:
        return kernel_body(seq_size // 2, *args)
    return plain_body(*args)


def solution(mesh):
    in_specs = (
        P(("groups", "seq"), None, "tensor"),
        P(("groups", "seq"), None, "tensor"),
        P(("groups", "seq"), None, "tensor"),
        P(("groups", "seq"), None, "tensor"),
        P("tensor", ("groups", "seq"), None),
        P("tensor", ("groups", "seq"), None),
        P("tensor", ("groups", "seq")),
        P("tensor", ("groups", "seq")),
        P(("groups", "seq"), None),
        P("groups"),
        P("tensor"),
        P("tensor", "seq"),
        P("tensor", "seq"),
        P("seq", "tensor"),
    )
    out_specs = P(("groups", "seq"), None, "tensor")
    body = functools.partial(choose_body, mesh.shape["seq"], mesh.shape["tensor"])
    return jax.shard_map(body, mesh=mesh, in_specs=in_specs, out_specs=out_specs, check_vma=False)
```

```python
import functools
import math

import jax
import jax.numpy as jnp
from jax import lax
from jax.experimental import pallas as pl
from jax.experimental.pallas import tpu as pltpu
from jax.sharding import PartitionSpec as P

D = 8192


NEG_FILL = -1e30
EPSILON = 1e-05
LOG2E = 1.4426950408889634


def combine_partials(earlier, later):
    shared_top = jnp.maximum(earlier[0], later[0])
    early_factor = jnp.exp2(earlier[0] - shared_top)
    late_factor = jnp.exp2(later[0] - shared_top)
    return (
        shared_top,
        earlier[1] * early_factor + later[1] * late_factor,
        earlier[2] * early_factor[..., None] + later[2] * late_factor[..., None],
    )


def masked_terms(scores, allowed_mask):
    row_top = jnp.ceil(jnp.max(jnp.where(allowed_mask, scores, NEG_FILL), axis=-1))
    exp_terms = jnp.where(allowed_mask, jnp.exp2(scores - row_top[..., None]), 0.0)
    return (row_top, exp_terms)


def plain_body(
    queries,
    fresh_keys,
    fresh_values,
    residual_in,
    cache_keys,
    cache_values,
    key_scales,
    value_scales,
    page_table,
    row_lengths,
    norm_gain,
    w_gate,
    w_up,
    w_down,
):
    local_rows = queries.shape[0]
    step_count = queries.shape[1]
    half_width = queries.shape[2]
    groups = cache_keys.shape[0]
    cache_span = cache_keys.shape[1]
    head_dim = cache_keys.shape[2]
    page_count = page_table.shape[1]
    block_size = cache_span // page_count
    heads_per = half_width // (groups * head_dim)
    inv_root = LOG2E / math.sqrt(head_dim)
    seq_index = lax.axis_index("seq")
    all_q, all_fk, all_fv, all_x = (
        lax.all_gather(queries, "seq", axis=0, tiled=True),
        lax.all_gather(fresh_keys, "seq", axis=0, tiled=True),
        lax.all_gather(fresh_values, "seq", axis=0, tiled=True),
        lax.all_gather(residual_in, "seq", axis=0, tiled=True),
    )
    all_rows = all_q.shape[0]
    offsets = jnp.arange(cache_span, dtype=jnp.int32)
    logical = seq_index * page_count + jnp.repeat(page_table[0], block_size)
    position = logical * block_size + offsets % block_size
    visible = position[None, :] < row_lengths[:, None]
    k_scale = jnp.repeat(key_scales, block_size, axis=1)
    v_scale = jnp.repeat(value_scales, block_size, axis=1)
    q_part = all_q.reshape(all_rows, step_count, groups, heads_per, head_dim)
    q_part = jnp.moveaxis(q_part, 2, 0)

    def per_group(operands):
        q_group, key_block, value_block, k_row, v_row = operands
        raw_scores = jnp.einsum(
            "nsqd,cd->nsqc", q_group, key_block, preferred_element_type=jnp.float32
        )
        scores = raw_scores * k_row * inv_root
        row_top, exp_terms = masked_terms(scores, visible[:, None, None, :])
        row_total = jnp.sum(exp_terms, axis=-1)
        weights = (exp_terms * v_row).astype(jnp.bfloat16)
        weighted = jnp.einsum(
            "nsqc,cd->nsqd", weights, value_block, preferred_element_type=jnp.float32
        )
        return (row_top, row_total, weighted)

    partial_value = lax.map(per_group, (q_part, cache_keys, cache_values, k_scale, v_scale))
    row_peak = lax.pmax(partial_value[0], "seq")
    factor = jnp.exp2(partial_value[0] - row_peak)
    row_total, weighted = lax.psum(
        (partial_value[1] * factor, partial_value[2] * factor[..., None]), "seq"
    )
    row_count = all_q.shape[0]
    fresh_row_count = all_q.shape[0]
    q_part = all_q.reshape(fresh_row_count, step_count, groups, heads_per, head_dim)
    k_part = all_fk.reshape(fresh_row_count, step_count, groups, head_dim)
    v_part = all_fv.reshape(fresh_row_count, step_count, groups, head_dim)
    raw_scores = jnp.einsum("nsgqd,ntgd->gnsqt", q_part, k_part, preferred_element_type=jnp.float32)
    scores = raw_scores * inv_root
    allowed = jnp.arange(step_count)[None, :] <= (0 + jnp.arange(step_count))[:, None]
    row_top, exp_terms = masked_terms(scores, allowed[None, None, :, None, :])
    fresh_row_total = jnp.sum(exp_terms, axis=-1)
    fresh_weighted = jnp.einsum(
        "gnsqt,ntgd->gnsqd",
        exp_terms.astype(jnp.bfloat16),
        v_part,
        preferred_element_type=jnp.float32,
    )
    joined = combine_partials(
        (row_peak, row_total, weighted), (row_top, fresh_row_total, fresh_weighted)
    )
    attention = joined[2] / joined[1][..., None]
    attention = jnp.moveaxis(attention, 0, 2).reshape(row_count, step_count, half_width)
    hidden_state = all_x.astype(jnp.float32) + attention
    square = lax.psum(jnp.sum(hidden_state * hidden_state, axis=-1), "tensor")
    inverse_rms = lax.rsqrt(square / D + EPSILON)
    normed = (hidden_state * inverse_rms[..., None] * norm_gain).astype(jnp.bfloat16)
    hidden_state, normed = (hidden_state, normed)
    own_state = lax.dynamic_slice_in_dim(hidden_state, seq_index * local_rows, local_rows, 0)
    flat_normed = normed.reshape(all_rows * step_count, half_width)
    gate_part = jnp.dot(flat_normed, w_gate, preferred_element_type=jnp.float32)
    up_part = jnp.dot(flat_normed, w_up, preferred_element_type=jnp.float32)
    gate_sums, up_sums = lax.psum((gate_part, up_part), "tensor")
    hidden = (jax.nn.silu(gate_sums) * up_sums).astype(jnp.bfloat16)
    down_sums = lax.psum_scatter(
        jnp.dot(hidden, w_down, preferred_element_type=jnp.float32),
        "seq",
        scatter_dimension=0,
        tiled=True,
    )
    return (own_state + down_sums.reshape(local_rows, step_count, half_width)).astype(jnp.bfloat16)


MESH = pl.DeviceIdType.MESH
FLOOR = -1e29
CHUNKS = 8
TILE = 256
LAG = 3


def layer_kernel(
    lines,
    q_ref,
    fk_ref,
    fv_ref,
    res_ref,
    lens_ref,
    ks_ref,
    vs_ref,
    pt_ref,
    gain_ref,
    ck_hbm,
    cv_hbm,
    wg_hbm,
    wu_hbm,
    wd_hbm,
    out_ref,
    kbuf,
    vbuf,
    wgu,
    wd,
    qbuf,
    lens,
    krow,
    vrow,
    prow,
    fkp,
    fvp,
    facc,
    fstat,
    part,
    stat,
    ypart,
    ystat,
    spart,
    sstat,
    zpart,
    zstat,
    hs,
    sq,
    nbuf,
    gacc,
    grecv,
    hbuf,
    dacc,
    dpart,
    dy,
    dsum,
    dz,
    local_sem,
    w_sem,
    qz_sem,
    qy_sem,
    py_sem,
    pz_sem,
    sq_sem,
    nz_sem,
    ny_sem,
    g_sem,
    h_sem,
    dy_sem,
    dz_sem,
):
    f32 = jnp.float32
    bf16 = jnp.bfloat16
    seq = lax.axis_index("seq")
    core = lax.axis_index("tensor")
    z, y = seq // 2, lax.rem(seq, 2)
    groups, span, hd = kbuf.shape
    local_rows, steps, width = q_ref.shape
    rows = local_rows * steps
    group_width = width // groups
    per = group_width // hd
    stack = per * rows
    pages = pt_ref.shape[1]
    page = span // pages
    inv_root = LOG2E / math.sqrt(hd)
    half = hbuf.shape[1] // 2
    pairs = groups * lines

    def line(d):
        return lax.rem(z + d, lines)

    def to_y():
        return {"seq": z * 2 + 1 - y}

    def to_z(zz):
        return {"seq": zz * 2 + y}

    def to_core():
        return {"tensor": 1 - core}

    def remote(src, dst, sems, send_at, recv_at, where):
        return pltpu.make_async_remote_copy(
            src_ref=src,
            dst_ref=dst,
            send_sem=sems.at[(0,) + send_at],
            recv_sem=sems.at[(1,) + recv_at],
            device_id=where,
            device_id_type=MESH,
        )

    cache_copies = [
        pltpu.make_async_copy(ck_hbm, kbuf, local_sem.at[0]),
        pltpu.make_async_copy(cv_hbm, vbuf, local_sem.at[1]),
    ]

    def gate_up_copies(p):
        piece = width // pairs
        at = pl.ds(pl.multiple_of(p * piece, 16), piece)
        return [
            pltpu.make_async_copy(
                src.at[at, pl.ds(h * half, half)],
                wgu.at[h, at, pl.ds(i * half, half)],
                w_sem.at[2 * i + h, p],
            )
            for i, src in enumerate((wg_hbm, wu_hbm))
            for h in range(2)
        ]

    def down_copy(p):
        piece = wd_hbm.shape[0] // pairs
        at = pl.ds(pl.multiple_of(p * piece, 16), piece)
        return pltpu.make_async_copy(wd_hbm.at[at], wd.at[at], w_sem.at[4, p])

    for copy in cache_copies:
        copy.start()

    barrier = pltpu.get_barrier_semaphore()
    peers = [to_y(), to_core()] + [to_z(line(d)) for d in range(1, lines)]
    for where in peers:
        pl.semaphore_signal(barrier, inc=1, device_id=where, device_id_type=MESH)

    flat_q = q_ref[...].reshape(rows, width)
    for g in range(groups):
        qbuf[g, y, z] = flat_q[:, g * group_width : (g + 1) * group_width]
    pl.semaphore_wait(barrier, len(peers))

    def gather_z(buf, sems, g, d):
        return remote(buf.at[g, y, z], buf.at[g, y, z], sems, (g, d), (g, z), to_z(line(d)))

    def gather_z_arrival(buf, sems, g, zz):
        return remote(buf.at[g, y, zz], buf.at[g, y, zz], sems, (g, 0), (g, zz), to_z(zz))

    def gather_y(buf, sems, g, zz):
        return remote(buf.at[g, y, zz], buf.at[g, y, zz], sems, (g, zz), (g, zz), to_y())

    def gather_y_arrival(buf, sems, g, zz):
        return remote(buf.at[g, 1 - y, zz], buf.at[g, 1 - y, zz], sems, (g, zz), (g, zz), to_y())

    for g in range(groups):
        gather_y(qbuf, qy_sem, g, z).start()
        for d in range(1, lines):
            gather_z(qbuf, qz_sem, g, d).start()

    row_of = lax.rem(lax.broadcasted_iota(jnp.int32, (stack, 1), 0), rows) // steps

    @pl.loop(0, 2 * lines)
    def _(k):
        yy, zz = lax.rem(k, 2), k // 2
        value = jnp.zeros((stack, 1), jnp.int32)
        for r in range(local_rows):
            value = jnp.where(row_of == r, lens_ref[k * local_rows + r], value)
        lens[yy, zz] = value

    owner = lax.broadcasted_iota(jnp.int32, (1, span), 1) // page
    within = lax.rem(lax.broadcasted_iota(jnp.int32, (1, span), 1), page)
    place = jnp.zeros((1, span), jnp.int32)
    for j in range(pages):
        place = jnp.where(owner == j, pt_ref[:, j : j + 1], place)
    prow[...] = (seq * pages + place) * page + within
    for g in range(groups):
        k_line = jnp.zeros((1, span), f32)
        v_line = jnp.zeros((1, span), f32)
        for j in range(pages):
            k_line = jnp.where(owner == j, ks_ref[g : g + 1, j : j + 1], k_line)
            v_line = jnp.where(owner == j, vs_ref[g : g + 1, j : j + 1], v_line)
        krow[g] = k_line * inv_root
        vrow[g] = v_line

    lane = lax.broadcasted_iota(jnp.int32, (stack, 128), 1)
    sublane = lax.broadcasted_iota(jnp.int32, (128, stack), 0)

    def stacked(block):
        return jnp.concatenate([block[:, j * hd : (j + 1) * hd] for j in range(per)], axis=0)

    def softmax_terms(scores):
        top = jnp.maximum(jnp.ceil(jnp.max(scores, axis=-1, keepdims=True)), FLOOR)
        terms = jnp.exp2(scores - top)
        total = jnp.sum(terms, axis=-1, keepdims=True)
        return terms, jnp.where(lane == 0, top, total).T[0:2]

    def columns_of(lines_in):
        table = jnp.zeros((128, stack), f32)
        for i, value in enumerate(lines_in):
            table = jnp.where(sublane == i, value, table)
        table = table.T
        return [table[:, i : i + 1] for i in range(len(lines_in))]

    fkp[...] = jnp.zeros_like(fkp)
    fvp[...] = jnp.zeros_like(fvp)
    fkp[0:rows] = fk_ref[...].reshape(rows, groups * hd)
    fvp[0:rows] = fv_ref[...].reshape(rows, groups * hd)
    slots = fkp.shape[0]
    token = lax.rem(lax.broadcasted_iota(jnp.int32, (stack, slots), 0), rows)
    key_token = lax.broadcasted_iota(jnp.int32, (stack, slots), 1)
    allowed = (token // steps == key_token // steps) & (key_token <= token)
    for g in range(groups):
        at = slice(g * hd, (g + 1) * hd)
        scores = lax.dot_general(
            stacked(qbuf.at[g, y, z]),
            fkp[:, at],
            (((1,), (1,)), ((), ())),
            preferred_element_type=f32,
        )
        terms, fstat[g] = softmax_terms(jnp.where(allowed, scores * inv_root, NEG_FILL))
        facc[g] = jnp.dot(terms.astype(bf16), fvp[:, at], preferred_element_type=f32)
    flat_res = res_ref[...].reshape(rows, width)
    for g in range(groups):
        hs[g] = flat_res[:, g * group_width : (g + 1) * group_width].astype(f32)
    gacc[...] = jnp.zeros_like(gacc)

    for copy in cache_copies:
        copy.wait()

    def attend(g, yy, zz):
        scores = lax.dot_general(
            stacked(qbuf.at[g, yy, zz]),
            kbuf[g],
            (((1,), (1,)), ((), ())),
            preferred_element_type=f32,
        )
        scores = jnp.where(prow[...] < lens[yy, zz], scores * krow[g], NEG_FILL)
        terms, stat[g, yy, zz] = softmax_terms(scores)
        part[g, yy, zz] = jnp.dot(
            (terms * vrow[g]).astype(bf16), vbuf[g], preferred_element_type=f32
        ).astype(bf16)

    def part_y(g, zz):
        src = (part.at[g, 1 - y, zz], stat.at[g, 1 - y, zz])
        dst = (ypart.at[g, zz], ystat.at[g, zz])
        return [remote(src[i], dst[i], py_sem, (i, g, zz), (i, g, zz), to_y()) for i in range(2)]

    def part_z(g, zz, at):
        src, dst = (spart.at[g, zz], sstat.at[g, zz]), (zpart.at[g, at], zstat.at[g, at])
        return [remote(src[i], dst[i], pz_sem, (i, g, zz), (i, g, at), to_z(zz)) for i in range(2)]

    def join(g, zz):
        for copy in part_y(g, zz):
            copy.wait_recv()
        first, second = stat[g, y, zz], ystat[g, zz]
        top = jnp.maximum(first[0:1], second[0:1])
        a, b = jnp.exp2(first[0:1] - top), jnp.exp2(second[0:1] - top)
        sstat[g, zz, 0:1] = top
        sstat[g, zz, 1:2] = first[1:2] * a + second[1:2] * b
        a, b = columns_of([a, b])
        spart[g, zz] = (part[g, y, zz].astype(f32) * a + ypart[g, zz].astype(f32) * b).astype(bf16)
        for copy in part_z(g, zz, z):
            copy.start()

    @pl.loop(0, 2 * pairs)
    def _(k):
        pair, other = k // 2, lax.rem(k, 2)
        g, d = pair // lines, lax.rem(pair, lines)
        zz = line(d)

        @pl.when(other == 0)
        def _():
            for copy in gate_up_copies(pair) + [down_copy(pair)]:
                copy.start()

        @pl.when((other == 0) & (d > 0))
        def _():
            gather_z_arrival(qbuf, qz_sem, g, zz).wait_recv()
            gather_y(qbuf, qy_sem, g, zz).start()

        @pl.when(other == 1)
        def _():
            gather_y_arrival(qbuf, qy_sem, g, zz).wait_recv()

        attend(g, lax.rem(y + other, 2), zz)

        @pl.when(other == 1)
        def _():
            for copy in part_y(g, zz):
                copy.start()

        late = pair + lines - LAG

        @pl.when((other == 1) & (late >= lines) & (lax.rem(late, lines) > 0))
        def _():
            join(late // lines - 1, line(lax.rem(late, lines)))

    for late in range(pairs - LAG, pairs):
        if late % lines:
            join(late // lines, line(late % lines))

    @pl.loop(0, groups)
    def _(g):
        for copy in part_y(g, z):
            copy.wait_recv()
        for d in range(1, lines):
            for copy in part_z(g, line(d), line(d)):
                copy.wait_recv()
        others = [line(d) for d in range(1, lines)]
        stats = [fstat[g], stat[g, y, z], ystat[g, z]] + [zstat[g, zz] for zz in others]
        parts = [facc[g], part[g, y, z], ypart[g, z]] + [zpart[g, zz] for zz in others]
        top = functools.reduce(jnp.maximum, [s[0:1] for s in stats])
        factors = [jnp.exp2(s[0:1] - top) for s in stats]
        total = sum(s[1:2] * f for s, f in zip(stats, factors))
        factors = columns_of([f / total for f in factors])
        attention = sum(p.astype(f32) * f for p, f in zip(parts, factors))
        square = jnp.zeros((rows, hd), f32)
        for j in range(per):
            at = slice(j * hd, (j + 1) * hd)
            state = hs[g, :, at] + attention[j * rows : (j + 1) * rows]
            hs[g, :, at] = state
            square += state * state
        sq[2 + g] = square

    square = sum(sq[2 + g] for g in range(groups))
    sq[0] = jnp.broadcast_to(jnp.sum(square, axis=-1, keepdims=True), (rows, 128))
    square_copy = remote(sq.at[0], sq.at[1], sq_sem, (0,), (0,), to_core())
    square_copy.start()
    square_copy.wait_recv()
    inverse = lax.rsqrt((sq[0] + sq[1])[:, 0:1] / (2 * width) + EPSILON)

    for g in range(groups):
        gain = gain_ref[:, g * group_width : (g + 1) * group_width]
        nbuf[g, y, z] = (hs[g] * inverse * gain).astype(bf16)
        gather_y(nbuf, ny_sem, g, z).start()
        for d in range(1, lines):
            gather_z(nbuf, nz_sem, g, d).start()

    def forward(g):
        for d in range(1, lines):
            gather_z_arrival(nbuf, nz_sem, g, line(d)).wait_recv()
            gather_y(nbuf, ny_sem, g, line(d)).start()

    @pl.loop(0, pairs)
    def _(p):
        for copy in gate_up_copies(p):
            copy.wait()

    all_rows = 2 * lines * rows
    tiles = 2 * half // TILE

    def swap(t):
        return remote(gacc.at[0, t], grecv.at[t], g_sem, (t,), (t,), to_core())

    def gate_up(g, slot, at):
        @pl.loop(0, tiles)
        def _(t):
            gacc[slot, t] += jnp.dot(
                nbuf[g].reshape(all_rows, group_width),
                wgu[
                    at,
                    pl.ds(pl.multiple_of(g * group_width, group_width), group_width),
                    pl.ds(pl.multiple_of(t * TILE, TILE), TILE),
                ],
                preferred_element_type=f32,
            )
            if slot == 0:

                @pl.when(g == groups - 1)
                def _():
                    swap(t).start()

    forward(0)

    @pl.loop(0, groups)
    def _(g):
        @pl.when(g < groups - 1)
        def _():
            forward(g + 1)

        for d in range(lines):
            gather_y_arrival(nbuf, ny_sem, g, line(d)).wait_recv()
        gate_up(g, 0, 1 - core)
        gate_up(g, 1, core)

    for t in range(tiles):
        swap(t).wait_recv()
    for b in range(half // 128):

        def summed(column):
            t, at = column // TILE, slice(column % TILE, column % TILE + 128)
            return gacc[1, t, :, at] + grecv[t, :, at]

        gate, up = summed(b * 128), summed(half + b * 128)
        hbuf[:, pl.ds(pl.multiple_of(core * half + b * 128, 128), 128)] = (
            gate / (1.0 + jnp.exp(-gate)) * up
        ).astype(bf16)

    def hidden_copy(at):
        both = hbuf.at[:, pl.ds(pl.multiple_of(at * half, 128), half)]
        return remote(both, both, h_sem, (0,), (0,), to_core())

    hidden_copy(core).start()

    @pl.loop(0, pairs)
    def _(p):
        down_copy(p).wait()

    hidden_copy(1 - core).wait_recv()

    chunk = width // CHUNKS

    def down_y(c):
        return remote(dpart.at[c], dy.at[c], dy_sem, (c,), (c,), to_y())

    def down_z(c, zz, at):
        return remote(dsum.at[c, zz], dz.at[c, at], dz_sem, (c, zz), (c, at), to_z(zz))

    def relay(c):
        down_y(c).wait_recv()
        for d in range(1, lines):
            zz = line(d)
            dsum[c, zz] = (dacc[c, y, zz] + dy[c, zz].astype(f32)).astype(bf16)
            down_z(c, zz, z).start()

    @pl.loop(0, CHUNKS)
    def _(c):
        for t in range(chunk // TILE):
            dacc[c, :, :, :, t * TILE : (t + 1) * TILE] = jnp.dot(
                hbuf[...],
                wd[:, pl.ds(pl.multiple_of(c * chunk + t * TILE, TILE), TILE)],
                preferred_element_type=f32,
            ).reshape(2, lines, rows, TILE)
        dpart[c] = dacc[c, 1 - y].astype(bf16)
        down_y(c).start()

        @pl.when(c >= LAG)
        def _():
            relay(c - LAG)

    for c in range(CHUNKS - LAG, CHUNKS):
        relay(c)
    for c in range(CHUNKS):
        g, first = c * chunk // group_width, c * chunk % group_width
        value = hs[g, :, first : first + chunk] + dacc[c, y, z] + dy[c, z].astype(f32)
        for d in range(1, lines):
            down_z(c, line(d), line(d)).wait_recv()
            value += dz[c, line(d)].astype(f32)
        out_ref[:, :, c * chunk : (c + 1) * chunk] = value.astype(out_ref.dtype).reshape(
            local_rows, steps, chunk
        )

    @pl.loop(0, groups)
    def _(g):
        for d in range(1, lines):
            gather_z(qbuf, qz_sem, g, d).wait_send()
            gather_z(nbuf, nz_sem, g, d).wait_send()
            for copy in part_z(g, line(d), z):
                copy.wait_send()
        for d in range(lines):
            gather_y(qbuf, qy_sem, g, line(d)).wait_send()
            gather_y(nbuf, ny_sem, g, line(d)).wait_send()
            for copy in part_y(g, line(d)):
                copy.wait_send()

    @pl.loop(0, CHUNKS)
    def _(c):
        down_y(c).wait_send()
        for d in range(1, lines):
            down_z(c, line(d), z).wait_send()

    for t in range(tiles):
        swap(t).wait_send()
    square_copy.wait_send()
    hidden_copy(core).wait_send()


def kernel_body(
    lines,
    queries,
    fresh_keys,
    fresh_values,
    residual_in,
    cache_keys,
    cache_values,
    key_scales,
    value_scales,
    page_table,
    row_lengths,
    norm_gain,
    w_gate,
    w_up,
    w_down,
):
    local_rows, steps, width = queries.shape
    groups, span, hd = cache_keys.shape
    rows = local_rows * steps
    group_width = width // groups
    stack = rows * group_width // hd
    fresh_width = fresh_keys.shape[2]
    hidden = w_gate.shape[1]
    half = hidden // 2
    tiles = hidden // TILE
    chunk = width // CHUNKS
    all_rows = 2 * lines * rows
    bf16, f32 = jnp.bfloat16, jnp.float32
    vmem = pl.BlockSpec(memory_space=pltpu.VMEM)
    smem = pl.BlockSpec(memory_space=pltpu.SMEM)
    anywhere = pl.BlockSpec(memory_space=pl.ANY)
    dma = pltpu.SemaphoreType.DMA
    return pl.pallas_call(
        functools.partial(layer_kernel, lines),
        out_shape=jax.ShapeDtypeStruct(queries.shape, bf16),
        in_specs=[vmem] * 4 + [smem] + [vmem] * 4 + [anywhere] * 5,
        out_specs=vmem,
        scratch_shapes=[
            pltpu.VMEM((groups, span, hd), bf16),
            pltpu.VMEM((groups, span, hd), bf16),
            pltpu.VMEM((2, width, 2 * half), bf16),
            pltpu.VMEM(w_down.shape, bf16),
            pltpu.VMEM((groups, 2, lines, rows, group_width), bf16),
            pltpu.VMEM((2, lines, stack, 1), jnp.int32),
            pltpu.VMEM((groups, 1, span), f32),
            pltpu.VMEM((groups, 1, span), f32),
            pltpu.VMEM((1, span), jnp.int32),
            pltpu.VMEM((128, fresh_width), bf16),
            pltpu.VMEM((128, fresh_width), bf16),
            pltpu.VMEM((groups, stack, hd), f32),
            pltpu.VMEM((groups, 2, stack), f32),
            pltpu.VMEM((groups, 2, lines, stack, hd), bf16),
            pltpu.VMEM((groups, 2, lines, 2, stack), f32),
            pltpu.VMEM((groups, lines, stack, hd), bf16),
            pltpu.VMEM((groups, lines, 2, stack), f32),
            pltpu.VMEM((groups, lines, stack, hd), bf16),
            pltpu.VMEM((groups, lines, 2, stack), f32),
            pltpu.VMEM((groups, lines, stack, hd), bf16),
            pltpu.VMEM((groups, lines, 2, stack), f32),
            pltpu.VMEM((groups, rows, group_width), f32),
            pltpu.VMEM((2 + groups, rows, 128), f32),
            pltpu.VMEM((groups, 2, lines, rows, group_width), bf16),
            pltpu.VMEM((2, tiles, all_rows, TILE), f32),
            pltpu.VMEM((tiles, all_rows, TILE), f32),
            pltpu.VMEM((all_rows, hidden), bf16),
            pltpu.VMEM((CHUNKS, 2, lines, rows, chunk), f32),
            pltpu.VMEM((CHUNKS, lines, rows, chunk), bf16),
            pltpu.VMEM((CHUNKS, lines, rows, chunk), bf16),
            pltpu.VMEM((CHUNKS, lines, rows, chunk), bf16),
            pltpu.VMEM((CHUNKS, lines, rows, chunk), bf16),
            dma((2,)),
            dma((5, groups * lines)),
            dma((2, groups, lines)),
            dma((2, groups, lines)),
            dma((2, 2, groups, lines)),
            dma((2, 2, groups, lines)),
            dma((2, 1)),
            dma((2, groups, lines)),
            dma((2, groups, lines)),
            dma((2, tiles)),
            dma((2, 1)),
            dma((2, CHUNKS)),
            dma((2, CHUNKS, lines)),
        ],
        compiler_params=pltpu.CompilerParams(
            collective_id=0, has_side_effects=True, vmem_limit_bytes=62 * 1024 * 1024
        ),
    )(
        queries,
        fresh_keys,
        fresh_values,
        residual_in,
        row_lengths,
        key_scales,
        value_scales,
        page_table,
        norm_gain.reshape(1, width),
        cache_keys,
        cache_values,
        w_gate,
        w_up,
        w_down,
    )


def choose_body(seq_size, cores, *args):
    local_rows, steps, width = args[0].shape
    groups, _, head_dim = args[4].shape
    rows, hidden = local_rows * steps, args[11].shape[1]
    stack = rows * width // (groups * head_dim)
    pairs = groups * (seq_size // 2)
    weights = 2 * 3 * width * hidden
    fits = (
        cores == 2
        and seq_size % 2 == 0
        and pairs > LAG
        and rows % 16 == 0
        and stack == 128
        and head_dim == 128
        and hidden % 256 == 0
        and hidden % (16 * pairs) == 0
        and width % (16 * pairs) == 0
        and width % (CHUNKS * TILE) == 0
        and CHUNKS % groups == 0
        and weights <= 44 * 1024 * 1024
    )
    if fits:
        return kernel_body(seq_size // 2, *args)
    return plain_body(*args)


def solution(mesh):
    in_specs = (
        P(("groups", "seq"), None, "tensor"),
        P(("groups", "seq"), None, "tensor"),
        P(("groups", "seq"), None, "tensor"),
        P(("groups", "seq"), None, "tensor"),
        P("tensor", ("groups", "seq"), None),
        P("tensor", ("groups", "seq"), None),
        P("tensor", ("groups", "seq")),
        P("tensor", ("groups", "seq")),
        P(("groups", "seq"), None),
        P("groups"),
        P("tensor"),
        P("tensor", "seq"),
        P("tensor", "seq"),
        P("seq", "tensor"),
    )
    out_specs = P(("groups", "seq"), None, "tensor")
    body = functools.partial(choose_body, mesh.shape["seq"], mesh.shape["tensor"])
    return jax.shard_map(body, mesh=mesh, in_specs=in_specs, out_specs=out_specs, check_vma=False)
```

```python
import functools
import math

import jax
import jax.numpy as jnp
from jax import lax
from jax.experimental import pallas as pl
from jax.experimental.pallas import tpu as pltpu
from jax.sharding import PartitionSpec as P

D = 8192


NEG_FILL = -1e30
EPSILON = 1e-05
LOG2E = 1.4426950408889634


def combine_partials(earlier, later):
    shared_top = jnp.maximum(earlier[0], later[0])
    early_factor = jnp.exp2(earlier[0] - shared_top)
    late_factor = jnp.exp2(later[0] - shared_top)
    return (
        shared_top,
        earlier[1] * early_factor + later[1] * late_factor,
        earlier[2] * early_factor[..., None] + later[2] * late_factor[..., None],
    )


def masked_terms(scores, allowed_mask):
    row_top = jnp.ceil(jnp.max(jnp.where(allowed_mask, scores, NEG_FILL), axis=-1))
    exp_terms = jnp.where(allowed_mask, jnp.exp2(scores - row_top[..., None]), 0.0)
    return (row_top, exp_terms)


def plain_body(
    queries,
    fresh_keys,
    fresh_values,
    residual_in,
    cache_keys,
    cache_values,
    key_scales,
    value_scales,
    page_table,
    row_lengths,
    norm_gain,
    w_gate,
    w_up,
    w_down,
):
    local_rows = queries.shape[0]
    step_count = queries.shape[1]
    half_width = queries.shape[2]
    groups = cache_keys.shape[0]
    cache_span = cache_keys.shape[1]
    head_dim = cache_keys.shape[2]
    page_count = page_table.shape[1]
    block_size = cache_span // page_count
    heads_per = half_width // (groups * head_dim)
    inv_root = LOG2E / math.sqrt(head_dim)
    seq_index = lax.axis_index("seq")
    all_q, all_fk, all_fv, all_x = (
        lax.all_gather(queries, "seq", axis=0, tiled=True),
        lax.all_gather(fresh_keys, "seq", axis=0, tiled=True),
        lax.all_gather(fresh_values, "seq", axis=0, tiled=True),
        lax.all_gather(residual_in, "seq", axis=0, tiled=True),
    )
    all_rows = all_q.shape[0]
    offsets = jnp.arange(cache_span, dtype=jnp.int32)
    logical = seq_index * page_count + jnp.repeat(page_table[0], block_size)
    position = logical * block_size + offsets % block_size
    visible = position[None, :] < row_lengths[:, None]
    k_scale = jnp.repeat(key_scales, block_size, axis=1)
    v_scale = jnp.repeat(value_scales, block_size, axis=1)
    q_part = all_q.reshape(all_rows, step_count, groups, heads_per, head_dim)
    q_part = jnp.moveaxis(q_part, 2, 0)

    def per_group(operands):
        q_group, key_block, value_block, k_row, v_row = operands
        raw_scores = jnp.einsum(
            "nsqd,cd->nsqc", q_group, key_block, preferred_element_type=jnp.float32
        )
        scores = raw_scores * k_row * inv_root
        row_top, exp_terms = masked_terms(scores, visible[:, None, None, :])
        row_total = jnp.sum(exp_terms, axis=-1)
        weights = (exp_terms * v_row).astype(jnp.bfloat16)
        weighted = jnp.einsum(
            "nsqc,cd->nsqd", weights, value_block, preferred_element_type=jnp.float32
        )
        return (row_top, row_total, weighted)

    partial_value = lax.map(per_group, (q_part, cache_keys, cache_values, k_scale, v_scale))
    row_peak = lax.pmax(partial_value[0], "seq")
    factor = jnp.exp2(partial_value[0] - row_peak)
    row_total, weighted = lax.psum(
        (partial_value[1] * factor, partial_value[2] * factor[..., None]), "seq"
    )
    row_count = all_q.shape[0]
    fresh_row_count = all_q.shape[0]
    q_part = all_q.reshape(fresh_row_count, step_count, groups, heads_per, head_dim)
    k_part = all_fk.reshape(fresh_row_count, step_count, groups, head_dim)
    v_part = all_fv.reshape(fresh_row_count, step_count, groups, head_dim)
    raw_scores = jnp.einsum("nsgqd,ntgd->gnsqt", q_part, k_part, preferred_element_type=jnp.float32)
    scores = raw_scores * inv_root
    allowed = jnp.arange(step_count)[None, :] <= (0 + jnp.arange(step_count))[:, None]
    row_top, exp_terms = masked_terms(scores, allowed[None, None, :, None, :])
    fresh_row_total = jnp.sum(exp_terms, axis=-1)
    fresh_weighted = jnp.einsum(
        "gnsqt,ntgd->gnsqd",
        exp_terms.astype(jnp.bfloat16),
        v_part,
        preferred_element_type=jnp.float32,
    )
    joined = combine_partials(
        (row_peak, row_total, weighted), (row_top, fresh_row_total, fresh_weighted)
    )
    attention = joined[2] / joined[1][..., None]
    attention = jnp.moveaxis(attention, 0, 2).reshape(row_count, step_count, half_width)
    hidden_state = all_x.astype(jnp.float32) + attention
    square = lax.psum(jnp.sum(hidden_state * hidden_state, axis=-1), "tensor")
    inverse_rms = lax.rsqrt(square / D + EPSILON)
    normed = (hidden_state * inverse_rms[..., None] * norm_gain).astype(jnp.bfloat16)
    hidden_state, normed = (hidden_state, normed)
    own_state = lax.dynamic_slice_in_dim(hidden_state, seq_index * local_rows, local_rows, 0)
    flat_normed = normed.reshape(all_rows * step_count, half_width)
    gate_part = jnp.dot(flat_normed, w_gate, preferred_element_type=jnp.float32)
    up_part = jnp.dot(flat_normed, w_up, preferred_element_type=jnp.float32)
    gate_sums, up_sums = lax.psum((gate_part, up_part), "tensor")
    hidden = (jax.nn.silu(gate_sums) * up_sums).astype(jnp.bfloat16)
    down_sums = lax.psum_scatter(
        jnp.dot(hidden, w_down, preferred_element_type=jnp.float32),
        "seq",
        scatter_dimension=0,
        tiled=True,
    )
    return (own_state + down_sums.reshape(local_rows, step_count, half_width)).astype(jnp.bfloat16)


MESH = pl.DeviceIdType.MESH
FLOOR = -1e29
CHUNKS = 8
TILE = 256
LAG = 3


def layer_kernel(
    lines,
    q_ref,
    fk_ref,
    fv_ref,
    res_ref,
    lens_ref,
    ks_ref,
    vs_ref,
    pt_ref,
    gain,
    ck_hbm,
    cv_hbm,
    wg_hbm,
    wu_hbm,
    wd_hbm,
    out_ref,
    kbuf,
    vbuf,
    wgu,
    wd,
    qbuf,
    lens,
    krow,
    vrow,
    prow,
    fkp,
    fvp,
    facc,
    fstat,
    part,
    stat,
    ypart,
    ystat,
    spart,
    sstat,
    zpart,
    zstat,
    hs,
    sq,
    ibuf,
    nbuf,
    gacc,
    grecv,
    hbuf,
    dacc,
    dpart,
    dy,
    dsum,
    dz,
    local_sem,
    w_sem,
    qz_sem,
    qy_sem,
    py_sem,
    pz_sem,
    sq_sem,
    iz_sem,
    iy_sem,
    nz_sem,
    ny_sem,
    g_sem,
    h_sem,
    dy_sem,
    dz_sem,
):
    f32 = jnp.float32
    bf16 = jnp.bfloat16
    seq = lax.axis_index("seq")
    core = lax.axis_index("tensor")
    z, y = seq // 2, lax.rem(seq, 2)
    groups, span, hd = kbuf.shape
    local_rows, steps, width = q_ref.shape
    rows = local_rows * steps
    group_width = width // groups
    per = group_width // hd
    stack = per * rows
    pages = pt_ref.shape[1]
    page = span // pages
    inv_root = LOG2E / math.sqrt(hd)
    half = hbuf.shape[1] // 2
    pairs = groups * lines

    def line(d):
        return lax.rem(z + d, lines)

    def to_y():
        return {"seq": z * 2 + 1 - y}

    def to_z(zz):
        return {"seq": zz * 2 + y}

    def to_core():
        return {"tensor": 1 - core}

    def remote(src, dst, sems, send_at, recv_at, where):
        return pltpu.make_async_remote_copy(
            src_ref=src,
            dst_ref=dst,
            send_sem=sems.at[(0,) + send_at],
            recv_sem=sems.at[(1,) + recv_at],
            device_id=where,
            device_id_type=MESH,
        )

    cache_copies = [
        pltpu.make_async_copy(ck_hbm, kbuf, local_sem.at[0]),
        pltpu.make_async_copy(cv_hbm, vbuf, local_sem.at[1]),
    ]

    def gate_up_copies(p):
        piece = width // pairs
        at = pl.ds(pl.multiple_of(p * piece, 16), piece)
        return [
            pltpu.make_async_copy(
                src.at[at, pl.ds(h * half, half)],
                wgu.at[h, at, pl.ds(i * half, half)],
                w_sem.at[2 * i + h, p],
            )
            for i, src in enumerate((wg_hbm, wu_hbm))
            for h in range(2)
        ]

    def down_copy(p):
        piece = wd_hbm.shape[0] // pairs
        at = pl.ds(pl.multiple_of(p * piece, 16), piece)
        return pltpu.make_async_copy(wd_hbm.at[at], wd.at[at], w_sem.at[4, p])

    for copy in cache_copies:
        copy.start()

    barrier = pltpu.get_barrier_semaphore()
    peers = [to_y(), to_core()] + [to_z(line(d)) for d in range(1, lines)]
    for where in peers:
        pl.semaphore_signal(barrier, inc=1, device_id=where, device_id_type=MESH)

    flat_q = q_ref[...].reshape(rows, width)
    for g in range(groups):
        qbuf[g, y, z] = flat_q[:, g * group_width : (g + 1) * group_width]
    pl.semaphore_wait(barrier, len(peers))

    def gather_z(buf, sems, g, d):
        return remote(buf.at[g, y, z], buf.at[g, y, z], sems, (g, d), (g, z), to_z(line(d)))

    def gather_z_arrival(buf, sems, g, zz):
        return remote(buf.at[g, y, zz], buf.at[g, y, zz], sems, (g, 0), (g, zz), to_z(zz))

    def gather_y(buf, sems, g, zz):
        return remote(buf.at[g, y, zz], buf.at[g, y, zz], sems, (g, zz), (g, zz), to_y())

    def gather_y_arrival(buf, sems, g, zz):
        return remote(buf.at[g, 1 - y, zz], buf.at[g, 1 - y, zz], sems, (g, zz), (g, zz), to_y())

    for g in range(groups):
        gather_y(qbuf, qy_sem, g, z).start()
        for d in range(1, lines):
            gather_z(qbuf, qz_sem, g, d).start()

    tall = lines * stack
    row_of = lax.rem(lax.broadcasted_iota(jnp.int32, (stack, 1), 0), rows) // steps
    for k in range(2 * lines):
        value = jnp.zeros((stack, 1), jnp.int32)
        for r in range(local_rows):
            value = jnp.where(row_of == r, lens_ref[k * local_rows + r], value)
        lens[k % 2, k // 2 * stack : (k // 2 + 1) * stack] = value

    owner = lax.broadcasted_iota(jnp.int32, (1, span), 1) // page
    within = lax.rem(lax.broadcasted_iota(jnp.int32, (1, span), 1), page)
    place = jnp.zeros((1, span), jnp.int32)
    for j in range(pages):
        place = jnp.where(owner == j, pt_ref[:, j : j + 1], place)
    prow[...] = (seq * pages + place) * page + within
    for g in range(groups):
        k_line = jnp.zeros((1, span), f32)
        v_line = jnp.zeros((1, span), f32)
        for j in range(pages):
            k_line = jnp.where(owner == j, ks_ref[g : g + 1, j : j + 1], k_line)
            v_line = jnp.where(owner == j, vs_ref[g : g + 1, j : j + 1], v_line)
        krow[g] = k_line * inv_root
        vrow[g] = v_line

    def stacked(block):
        return [block[:, j * hd : (j + 1) * hd] for j in range(per)]

    def softmax_terms(scores):
        top = jnp.maximum(jnp.ceil(jnp.max(scores, axis=-1, keepdims=True)), FLOOR)
        terms = jnp.exp2(scores - top)
        total = jnp.sum(terms, axis=-1, keepdims=True)
        lane = lax.broadcasted_iota(jnp.int32, (scores.shape[0], 128), 1)
        return terms, jnp.where(lane == 0, top, total).T[0:2]

    def columns_of(lines_in):
        shape = (128, lines_in[0].shape[1])
        sublane = lax.broadcasted_iota(jnp.int32, shape, 0)
        table = jnp.zeros(shape, f32)
        for i, value in enumerate(lines_in):
            table = jnp.where(sublane == i, value, table)
        table = table.T
        return [table[:, i : i + 1] for i in range(len(lines_in))]

    fkp[...] = jnp.zeros_like(fkp)
    fvp[...] = jnp.zeros_like(fvp)
    fkp[0:rows] = fk_ref[...].reshape(rows, groups * hd)
    fvp[0:rows] = fv_ref[...].reshape(rows, groups * hd)
    slots = fkp.shape[0]
    token = lax.rem(lax.broadcasted_iota(jnp.int32, (stack, slots), 0), rows)
    key_token = lax.broadcasted_iota(jnp.int32, (stack, slots), 1)
    allowed = (token // steps == key_token // steps) & (key_token <= token)
    for g in range(groups):
        at = slice(g * hd, (g + 1) * hd)
        scores = lax.dot_general(
            jnp.concatenate(stacked(qbuf.at[g, y, z]), axis=0),
            fkp[:, at],
            (((1,), (1,)), ((), ())),
            preferred_element_type=f32,
        )
        terms, fstat[g] = softmax_terms(jnp.where(allowed, scores * inv_root, NEG_FILL))
        facc[g] = jnp.dot(terms.astype(bf16), fvp[:, at], preferred_element_type=f32)
    flat_res = res_ref[...].reshape(rows, width)
    for g in range(groups):
        hs[g] = flat_res[:, g * group_width : (g + 1) * group_width].astype(f32)
    gacc[...] = jnp.zeros_like(gacc)

    for copy in cache_copies:
        copy.wait()

    def attend(g, yy):
        heads = [head for zz in range(lines) for head in stacked(qbuf.at[g, yy, zz])]
        scores = lax.dot_general(
            jnp.concatenate(heads, axis=0),
            kbuf[g],
            (((1,), (1,)), ((), ())),
            preferred_element_type=f32,
        )
        scores = jnp.where(prow[...] < lens[yy], scores * krow[g], NEG_FILL)
        terms, stat[g, yy] = softmax_terms(scores)
        part[g, yy] = (
            jnp.dot((terms * vrow[g]).astype(bf16), vbuf[g], preferred_element_type=f32)
            .astype(bf16)
            .reshape(lines, stack, hd)
        )

    def part_y(g):
        src = (part.at[g, 1 - y], stat.at[g, 1 - y])
        dst = (ypart.at[g], ystat.at[g])
        return [remote(src[i], dst[i], py_sem, (i, g), (i, g), to_y()) for i in range(2)]

    def part_z(g, zz, at):
        src, dst = (spart.at[g, zz], sstat.at[g, zz]), (zpart.at[g, at], zstat.at[g, at])
        return [remote(src[i], dst[i], pz_sem, (i, g, zz), (i, g, at), to_z(zz)) for i in range(2)]

    def join(g):
        for copy in part_y(g):
            copy.wait_recv()
        first, second = stat[g, y], ystat[g]
        top = jnp.maximum(first[0:1], second[0:1])
        a, b = jnp.exp2(first[0:1] - top), jnp.exp2(second[0:1] - top)
        total = first[1:2] * a + second[1:2] * b
        for zz in range(lines):
            at = slice(zz * stack, (zz + 1) * stack)
            sstat[g, zz, 0:1] = top[:, at]
            sstat[g, zz, 1:2] = total[:, at]
        a, b = columns_of([a, b])
        joined = (
            part[g, y].reshape(tall, hd).astype(f32) * a
            + ypart[g].reshape(tall, hd).astype(f32) * b
        )
        spart[g] = joined.astype(bf16).reshape(lines, stack, hd)
        for d in range(1, lines):
            for copy in part_z(g, line(d), z):
                copy.start()

    def finish(g):
        others = [line(d) for d in range(1, lines)]
        for zz in others:
            for copy in part_z(g, zz, zz):
                copy.wait_recv()
        mine = pl.ds(pl.multiple_of(z * stack, stack), stack)
        stats = [fstat[g], stat[g, y, :, mine], ystat[g, :, mine]] + [zstat[g, zz] for zz in others]
        parts = [facc[g], part[g, y, z], ypart[g, z]] + [zpart[g, zz] for zz in others]
        top = functools.reduce(jnp.maximum, [s[0:1] for s in stats])
        factors = [jnp.exp2(s[0:1] - top) for s in stats]
        total = sum(s[1:2] * f for s, f in zip(stats, factors))
        factors = columns_of([f / total for f in factors])
        attention = sum(p.astype(f32) * f for p, f in zip(parts, factors))
        square = jnp.zeros((rows, hd), f32)
        for j in range(per):
            at = slice(j * hd, (j + 1) * hd)
            state = hs[g, :, at] + attention[j * rows : (j + 1) * rows]
            hs[g, :, at] = state
            square += state * state
        sq[2 + g] = square
        nbuf[g, y, z] = (hs[g] * gain[g]).astype(bf16)
        gather_y(nbuf, ny_sem, g, z).start()
        for d in range(1, lines):
            gather_z(nbuf, nz_sem, g, d).start()

    def forward(buf, z_sems, y_sems, g):
        for d in range(1, lines):
            gather_z_arrival(buf, z_sems, g, line(d)).wait_recv()
            gather_y(buf, y_sems, g, line(d)).start()

    def arrivals(buf, y_sems, g):
        for d in range(lines):
            gather_y_arrival(buf, y_sems, g, line(d)).wait_recv()

    square_copy = remote(sq.at[0], sq.at[1], sq_sem, (0,), (0,), to_core())

    all_rows = 2 * lines * rows
    tiles = 2 * half // TILE

    def swap(t):
        return remote(gacc.at[0, t], grecv.at[t], g_sem, (t,), (t,), to_core())

    def gate_up(g):
        for slot, at in ((0, 1 - core), (1, core)):
            for t in range(tiles):
                gacc[slot, t] += jnp.dot(
                    nbuf[g].reshape(all_rows, group_width),
                    wgu[
                        at,
                        pl.ds(pl.multiple_of(g * group_width, group_width), group_width),
                        t * TILE : (t + 1) * TILE,
                    ],
                    preferred_element_type=f32,
                )
            if slot == 0:

                @pl.when(g == groups - 1)
                def _():
                    for t in range(tiles):
                        swap(t).start()

    forward(qbuf, qz_sem, qy_sem, 0)

    @pl.loop(0, groups + 4)
    def _(i):
        @pl.when(i < groups)
        def _():
            for p in range(lines):
                for copy in gate_up_copies(i * lines + p):
                    copy.start()

        @pl.when(i >= 4)
        def _():
            for p in range(lines):
                down_copy((i - 4) * lines + p).start()

        @pl.when(i + 1 < groups)
        def _():
            forward(qbuf, qz_sem, qy_sem, i + 1)

        @pl.when((i >= 3) & (i < groups + 3))
        def _():
            forward(nbuf, nz_sem, ny_sem, i - 3)

        @pl.when(i == groups + 2)
        def _():
            square_copy.wait_recv()
            inverse = lax.rsqrt((sq[0] + sq[1]) / (2 * width) + EPSILON)
            ibuf[0, y, z] = inverse
            gather_y(ibuf, iy_sem, 0, z).start()
            for d in range(1, lines):
                gather_z(ibuf, iz_sem, 0, d).start()

        @pl.when(i == groups + 3)
        def _():
            forward(ibuf, iz_sem, iy_sem, 0)

        @pl.when((i >= 1) & (i < groups + 1))
        def _():
            join(i - 1)

        @pl.when((i >= 2) & (i < groups + 2))
        def _():
            finish(i - 2)

        @pl.when(i == groups + 1)
        def _():
            square = sum(sq[2 + g] for g in range(groups))
            sq[0] = jnp.broadcast_to(jnp.sum(square, axis=-1, keepdims=True), (rows, 128))
            square_copy.start()

        @pl.when(i < groups)
        def _():
            attend(i, y)
            arrivals(qbuf, qy_sem, i)
            attend(i, 1 - y)
            for copy in part_y(i):
                copy.start()

        @pl.when(i >= 4)
        def _():
            for p in range(lines):
                for copy in gate_up_copies((i - 4) * lines + p):
                    copy.wait()
            arrivals(nbuf, ny_sem, i - 4)
            gate_up(i - 4)

    arrivals(ibuf, iy_sem, 0)
    for t in range(tiles):
        swap(t).wait_recv()
    for b in range(half // 128):
        inverse = ibuf[0].reshape(all_rows, 128)

        def summed(column):
            t, at = column // TILE, slice(column % TILE, column % TILE + 128)
            return (gacc[1, t, :, at] + grecv[t, :, at]) * inverse

        gate, up = summed(b * 128), summed(half + b * 128)
        hbuf[:, pl.ds(pl.multiple_of(core * half + b * 128, 128), 128)] = (
            gate / (1.0 + jnp.exp(-gate)) * up
        ).astype(bf16)

    def hidden_copy(at):
        both = hbuf.at[:, pl.ds(pl.multiple_of(at * half, 128), half)]
        return remote(both, both, h_sem, (0,), (0,), to_core())

    hidden_copy(core).start()

    @pl.loop(0, pairs)
    def _(p):
        down_copy(p).wait()

    hidden_copy(1 - core).wait_recv()

    chunk = width // CHUNKS

    def down_y(c):
        return remote(dpart.at[c], dy.at[c], dy_sem, (c,), (c,), to_y())

    def down_z(c, zz, at):
        return remote(dsum.at[c, zz], dz.at[c, at], dz_sem, (c, zz), (c, at), to_z(zz))

    def relay(c):
        down_y(c).wait_recv()
        for d in range(1, lines):
            zz = line(d)
            dsum[c, zz] = (dacc[c, y, zz] + dy[c, zz].astype(f32)).astype(bf16)
            down_z(c, zz, z).start()

    @pl.loop(0, CHUNKS)
    def _(c):
        for t in range(chunk // TILE):
            dacc[c, :, :, :, t * TILE : (t + 1) * TILE] = jnp.dot(
                hbuf[...],
                wd[:, pl.ds(pl.multiple_of(c * chunk + t * TILE, TILE), TILE)],
                preferred_element_type=f32,
            ).reshape(2, lines, rows, TILE)
        dpart[c] = dacc[c, 1 - y].astype(bf16)
        down_y(c).start()

        @pl.when(c >= LAG)
        def _():
            relay(c - LAG)

    for c in range(CHUNKS - LAG, CHUNKS):
        relay(c)
    for c in range(CHUNKS):
        g, first = c * chunk // group_width, c * chunk % group_width
        value = hs[g, :, first : first + chunk] + dacc[c, y, z] + dy[c, z].astype(f32)
        for d in range(1, lines):
            down_z(c, line(d), line(d)).wait_recv()
            value += dz[c, line(d)].astype(f32)
        out_ref[:, :, c * chunk : (c + 1) * chunk] = value.astype(out_ref.dtype).reshape(
            local_rows, steps, chunk
        )

    @pl.loop(0, groups)
    def _(g):
        for d in range(1, lines):
            gather_z(qbuf, qz_sem, g, d).wait_send()
            gather_z(nbuf, nz_sem, g, d).wait_send()
            for copy in part_z(g, line(d), z):
                copy.wait_send()
        for d in range(lines):
            gather_y(qbuf, qy_sem, g, line(d)).wait_send()
            gather_y(nbuf, ny_sem, g, line(d)).wait_send()
        for copy in part_y(g):
            copy.wait_send()

    @pl.loop(0, CHUNKS)
    def _(c):
        down_y(c).wait_send()
        for d in range(1, lines):
            down_z(c, line(d), z).wait_send()

    for t in range(tiles):
        swap(t).wait_send()
    for d in range(1, lines):
        gather_z(ibuf, iz_sem, 0, d).wait_send()
    for d in range(lines):
        gather_y(ibuf, iy_sem, 0, line(d)).wait_send()
    square_copy.wait_send()
    hidden_copy(core).wait_send()


def kernel_body(
    lines,
    queries,
    fresh_keys,
    fresh_values,
    residual_in,
    cache_keys,
    cache_values,
    key_scales,
    value_scales,
    page_table,
    row_lengths,
    norm_gain,
    w_gate,
    w_up,
    w_down,
):
    local_rows, steps, width = queries.shape
    groups, span, hd = cache_keys.shape
    rows = local_rows * steps
    group_width = width // groups
    stack = rows * group_width // hd
    fresh_width = fresh_keys.shape[2]
    hidden = w_gate.shape[1]
    half = hidden // 2
    tiles = hidden // TILE
    chunk = width // CHUNKS
    all_rows = 2 * lines * rows
    bf16, f32 = jnp.bfloat16, jnp.float32
    vmem = pl.BlockSpec(memory_space=pltpu.VMEM)
    smem = pl.BlockSpec(memory_space=pltpu.SMEM)
    anywhere = pl.BlockSpec(memory_space=pl.ANY)
    dma = pltpu.SemaphoreType.DMA
    return pl.pallas_call(
        functools.partial(layer_kernel, lines),
        out_shape=jax.ShapeDtypeStruct(queries.shape, bf16),
        in_specs=[vmem] * 4 + [smem] + [vmem] * 4 + [anywhere] * 5,
        out_specs=vmem,
        scratch_shapes=[
            pltpu.VMEM((groups, span, hd), bf16),
            pltpu.VMEM((groups, span, hd), bf16),
            pltpu.VMEM((2, width, 2 * half), bf16),
            pltpu.VMEM(w_down.shape, bf16),
            pltpu.VMEM((groups, 2, lines, rows, group_width), bf16),
            pltpu.VMEM((2, lines * stack, 1), jnp.int32),
            pltpu.VMEM((groups, 1, span), f32),
            pltpu.VMEM((groups, 1, span), f32),
            pltpu.VMEM((1, span), jnp.int32),
            pltpu.VMEM((128, fresh_width), bf16),
            pltpu.VMEM((128, fresh_width), bf16),
            pltpu.VMEM((groups, stack, hd), f32),
            pltpu.VMEM((groups, 2, stack), f32),
            pltpu.VMEM((groups, 2, lines, stack, hd), bf16),
            pltpu.VMEM((groups, 2, 2, lines * stack), f32),
            pltpu.VMEM((groups, lines, stack, hd), bf16),
            pltpu.VMEM((groups, 2, lines * stack), f32),
            pltpu.VMEM((groups, lines, stack, hd), bf16),
            pltpu.VMEM((groups, lines, 2, stack), f32),
            pltpu.VMEM((groups, lines, stack, hd), bf16),
            pltpu.VMEM((groups, lines, 2, stack), f32),
            pltpu.VMEM((groups, rows, group_width), f32),
            pltpu.VMEM((2 + groups, rows, 128), f32),
            pltpu.VMEM((1, 2, lines, rows, 128), f32),
            pltpu.VMEM((groups, 2, lines, rows, group_width), bf16),
            pltpu.VMEM((2, tiles, all_rows, TILE), f32),
            pltpu.VMEM((tiles, all_rows, TILE), f32),
            pltpu.VMEM((all_rows, hidden), bf16),
            pltpu.VMEM((CHUNKS, 2, lines, rows, chunk), f32),
            pltpu.VMEM((CHUNKS, lines, rows, chunk), bf16),
            pltpu.VMEM((CHUNKS, lines, rows, chunk), bf16),
            pltpu.VMEM((CHUNKS, lines, rows, chunk), bf16),
            pltpu.VMEM((CHUNKS, lines, rows, chunk), bf16),
            dma((2,)),
            dma((5, groups * lines)),
            dma((2, groups, lines)),
            dma((2, groups, lines)),
            dma((2, 2, groups)),
            dma((2, 2, groups, lines)),
            dma((2, 1)),
            dma((2, 1, lines)),
            dma((2, 1, lines)),
            dma((2, groups, lines)),
            dma((2, groups, lines)),
            dma((2, tiles)),
            dma((2, 1)),
            dma((2, CHUNKS)),
            dma((2, CHUNKS, lines)),
        ],
        compiler_params=pltpu.CompilerParams(
            collective_id=0, has_side_effects=True, vmem_limit_bytes=62 * 1024 * 1024
        ),
    )(
        queries,
        fresh_keys,
        fresh_values,
        residual_in,
        row_lengths,
        key_scales,
        value_scales,
        page_table,
        norm_gain.reshape(groups, 1, group_width),
        cache_keys,
        cache_values,
        w_gate,
        w_up,
        w_down,
    )


def choose_body(seq_size, cores, *args):
    local_rows, steps, width = args[0].shape
    groups, _, head_dim = args[4].shape
    rows, hidden = local_rows * steps, args[11].shape[1]
    stack = rows * width // (groups * head_dim)
    pairs = groups * (seq_size // 2)
    weights = 2 * 3 * width * hidden
    fits = (
        cores == 2
        and seq_size % 2 == 0
        and rows % 16 == 0
        and stack == 128
        and head_dim == 128
        and hidden % 256 == 0
        and hidden % (16 * pairs) == 0
        and width % (16 * pairs) == 0
        and width % (CHUNKS * TILE) == 0
        and CHUNKS % groups == 0
        and weights <= 44 * 1024 * 1024
    )
    if fits:
        return kernel_body(seq_size // 2, *args)
    return plain_body(*args)


def solution(mesh):
    in_specs = (
        P(("groups", "seq"), None, "tensor"),
        P(("groups", "seq"), None, "tensor"),
        P(("groups", "seq"), None, "tensor"),
        P(("groups", "seq"), None, "tensor"),
        P("tensor", ("groups", "seq"), None),
        P("tensor", ("groups", "seq"), None),
        P("tensor", ("groups", "seq")),
        P("tensor", ("groups", "seq")),
        P(("groups", "seq"), None),
        P("groups"),
        P("tensor"),
        P("tensor", "seq"),
        P("tensor", "seq"),
        P("seq", "tensor"),
    )
    out_specs = P(("groups", "seq"), None, "tensor")
    body = functools.partial(choose_body, mesh.shape["seq"], mesh.shape["tensor"])
    return jax.shard_map(body, mesh=mesh, in_specs=in_specs, out_specs=out_specs, check_vma=False)
```

```python
import functools
import math

import jax
import jax.numpy as jnp
from jax import lax
from jax.experimental import pallas as pl
from jax.experimental.pallas import tpu as pltpu
from jax.sharding import PartitionSpec as P

D = 8192


NEG_FILL = -1e30
EPSILON = 1e-05
LOG2E = 1.4426950408889634


def combine_partials(earlier, later):
    shared_top = jnp.maximum(earlier[0], later[0])
    early_factor = jnp.exp2(earlier[0] - shared_top)
    late_factor = jnp.exp2(later[0] - shared_top)
    return (
        shared_top,
        earlier[1] * early_factor + later[1] * late_factor,
        earlier[2] * early_factor[..., None] + later[2] * late_factor[..., None],
    )


def masked_terms(scores, allowed_mask):
    row_top = jnp.ceil(jnp.max(jnp.where(allowed_mask, scores, NEG_FILL), axis=-1))
    exp_terms = jnp.where(allowed_mask, jnp.exp2(scores - row_top[..., None]), 0.0)
    return (row_top, exp_terms)


def plain_body(
    queries,
    fresh_keys,
    fresh_values,
    residual_in,
    cache_keys,
    cache_values,
    key_scales,
    value_scales,
    page_table,
    row_lengths,
    norm_gain,
    w_gate,
    w_up,
    w_down,
):
    local_rows = queries.shape[0]
    step_count = queries.shape[1]
    half_width = queries.shape[2]
    groups = cache_keys.shape[0]
    cache_span = cache_keys.shape[1]
    head_dim = cache_keys.shape[2]
    page_count = page_table.shape[1]
    block_size = cache_span // page_count
    heads_per = half_width // (groups * head_dim)
    inv_root = LOG2E / math.sqrt(head_dim)
    seq_index = lax.axis_index("seq")
    all_q, all_fk, all_fv, all_x = (
        lax.all_gather(queries, "seq", axis=0, tiled=True),
        lax.all_gather(fresh_keys, "seq", axis=0, tiled=True),
        lax.all_gather(fresh_values, "seq", axis=0, tiled=True),
        lax.all_gather(residual_in, "seq", axis=0, tiled=True),
    )
    all_rows = all_q.shape[0]
    offsets = jnp.arange(cache_span, dtype=jnp.int32)
    logical = seq_index * page_count + jnp.repeat(page_table[0], block_size)
    position = logical * block_size + offsets % block_size
    visible = position[None, :] < row_lengths[:, None]
    k_scale = jnp.repeat(key_scales, block_size, axis=1)
    v_scale = jnp.repeat(value_scales, block_size, axis=1)
    q_part = all_q.reshape(all_rows, step_count, groups, heads_per, head_dim)
    q_part = jnp.moveaxis(q_part, 2, 0)

    def per_group(operands):
        q_group, key_block, value_block, k_row, v_row = operands
        raw_scores = jnp.einsum(
            "nsqd,cd->nsqc", q_group, key_block, preferred_element_type=jnp.float32
        )
        scores = raw_scores * k_row * inv_root
        row_top, exp_terms = masked_terms(scores, visible[:, None, None, :])
        row_total = jnp.sum(exp_terms, axis=-1)
        weights = (exp_terms * v_row).astype(jnp.bfloat16)
        weighted = jnp.einsum(
            "nsqc,cd->nsqd", weights, value_block, preferred_element_type=jnp.float32
        )
        return (row_top, row_total, weighted)

    partial_value = lax.map(per_group, (q_part, cache_keys, cache_values, k_scale, v_scale))
    row_peak = lax.pmax(partial_value[0], "seq")
    factor = jnp.exp2(partial_value[0] - row_peak)
    row_total, weighted = lax.psum(
        (partial_value[1] * factor, partial_value[2] * factor[..., None]), "seq"
    )
    row_count = all_q.shape[0]
    fresh_row_count = all_q.shape[0]
    q_part = all_q.reshape(fresh_row_count, step_count, groups, heads_per, head_dim)
    k_part = all_fk.reshape(fresh_row_count, step_count, groups, head_dim)
    v_part = all_fv.reshape(fresh_row_count, step_count, groups, head_dim)
    raw_scores = jnp.einsum("nsgqd,ntgd->gnsqt", q_part, k_part, preferred_element_type=jnp.float32)
    scores = raw_scores * inv_root
    allowed = jnp.arange(step_count)[None, :] <= (0 + jnp.arange(step_count))[:, None]
    row_top, exp_terms = masked_terms(scores, allowed[None, None, :, None, :])
    fresh_row_total = jnp.sum(exp_terms, axis=-1)
    fresh_weighted = jnp.einsum(
        "gnsqt,ntgd->gnsqd",
        exp_terms.astype(jnp.bfloat16),
        v_part,
        preferred_element_type=jnp.float32,
    )
    joined = combine_partials(
        (row_peak, row_total, weighted), (row_top, fresh_row_total, fresh_weighted)
    )
    attention = joined[2] / joined[1][..., None]
    attention = jnp.moveaxis(attention, 0, 2).reshape(row_count, step_count, half_width)
    hidden_state = all_x.astype(jnp.float32) + attention
    square = lax.psum(jnp.sum(hidden_state * hidden_state, axis=-1), "tensor")
    inverse_rms = lax.rsqrt(square / D + EPSILON)
    normed = (hidden_state * inverse_rms[..., None] * norm_gain).astype(jnp.bfloat16)
    hidden_state, normed = (hidden_state, normed)
    own_state = lax.dynamic_slice_in_dim(hidden_state, seq_index * local_rows, local_rows, 0)
    flat_normed = normed.reshape(all_rows * step_count, half_width)
    gate_part = jnp.dot(flat_normed, w_gate, preferred_element_type=jnp.float32)
    up_part = jnp.dot(flat_normed, w_up, preferred_element_type=jnp.float32)
    gate_sums, up_sums = lax.psum((gate_part, up_part), "tensor")
    hidden = (jax.nn.silu(gate_sums) * up_sums).astype(jnp.bfloat16)
    down_sums = lax.psum_scatter(
        jnp.dot(hidden, w_down, preferred_element_type=jnp.float32),
        "seq",
        scatter_dimension=0,
        tiled=True,
    )
    return (own_state + down_sums.reshape(local_rows, step_count, half_width)).astype(jnp.bfloat16)


MESH = pl.DeviceIdType.MESH
FLOOR = -1e29
CHUNKS = 8
TILE = 256
LAG = 3


def layer_kernel(
    lines,
    q_ref,
    fk_ref,
    fv_ref,
    res_ref,
    lens_ref,
    ks_ref,
    vs_ref,
    pt_ref,
    gain,
    ck_hbm,
    cv_hbm,
    wg_hbm,
    wu_hbm,
    wd_hbm,
    out_ref,
    kbuf,
    vbuf,
    wgu,
    wd,
    qbuf,
    lens,
    krow,
    vrow,
    prow,
    fkp,
    fvp,
    facc,
    fstat,
    part,
    stat,
    ypart,
    ystat,
    spart,
    sstat,
    zpart,
    zstat,
    hs,
    sq,
    ibuf,
    nbuf,
    gacc,
    grecv,
    hbuf,
    dacc,
    dpart,
    dy,
    dsum,
    dz,
    local_sem,
    w_sem,
    qz_sem,
    qy_sem,
    py_sem,
    pz_sem,
    sq_sem,
    iz_sem,
    iy_sem,
    nz_sem,
    ny_sem,
    g_sem,
    h_sem,
    dy_sem,
    dz_sem,
):
    f32 = jnp.float32
    bf16 = jnp.bfloat16
    seq = lax.axis_index("seq")
    core = lax.axis_index("tensor")
    z, y = seq // 2, lax.rem(seq, 2)
    groups, span, hd = kbuf.shape
    local_rows, steps, width = q_ref.shape
    rows = local_rows * steps
    group_width = width // groups
    per = group_width // hd
    stack = per * rows
    pages = pt_ref.shape[1]
    page = span // pages
    inv_root = LOG2E / math.sqrt(hd)
    half = hbuf.shape[1] // 2
    pairs = groups * lines

    def line(d):
        return lax.rem(z + d, lines)

    def to_y():
        return {"seq": z * 2 + 1 - y}

    def to_z(zz):
        return {"seq": zz * 2 + y}

    def to_core():
        return {"tensor": 1 - core}

    def remote(src, dst, sems, send_at, recv_at, where):
        return pltpu.make_async_remote_copy(
            src_ref=src,
            dst_ref=dst,
            send_sem=sems.at[(0,) + send_at],
            recv_sem=sems.at[(1,) + recv_at],
            device_id=where,
            device_id_type=MESH,
        )

    cache_copies = [
        pltpu.make_async_copy(ck_hbm, kbuf, local_sem.at[0]),
        pltpu.make_async_copy(cv_hbm, vbuf, local_sem.at[1]),
    ]

    def gate_up_copies(p):
        piece = width // pairs
        at = pl.ds(pl.multiple_of(p * piece, 16), piece)
        return [
            pltpu.make_async_copy(
                src.at[at, pl.ds(h * half, half)],
                wgu.at[h, at, pl.ds(i * half, half)],
                w_sem.at[2 * i + h, p],
            )
            for i, src in enumerate((wg_hbm, wu_hbm))
            for h in range(2)
        ]

    def down_copy(p):
        piece = wd_hbm.shape[0] // pairs
        at = pl.ds(pl.multiple_of(p * piece, 16), piece)
        return pltpu.make_async_copy(wd_hbm.at[at], wd.at[at], w_sem.at[4, p])

    for copy in cache_copies:
        copy.start()

    barrier = pltpu.get_barrier_semaphore()
    peers = [to_y(), to_core()] + [to_z(line(d)) for d in range(1, lines)]
    for where in peers:
        pl.semaphore_signal(barrier, inc=1, device_id=where, device_id_type=MESH)

    flat_q = q_ref[...].reshape(rows, width)
    for g in range(groups):
        qbuf[g, y, z] = flat_q[:, g * group_width : (g + 1) * group_width]
    pl.semaphore_wait(barrier, len(peers))

    def gather_z(buf, sems, g, d):
        return remote(buf.at[g, y, z], buf.at[g, y, z], sems, (g, d), (g, z), to_z(line(d)))

    def gather_z_arrival(buf, sems, g, zz):
        return remote(buf.at[g, y, zz], buf.at[g, y, zz], sems, (g, 0), (g, zz), to_z(zz))

    def gather_y(buf, sems, g, zz):
        return remote(buf.at[g, y, zz], buf.at[g, y, zz], sems, (g, zz), (g, zz), to_y())

    def gather_y_arrival(buf, sems, g, zz):
        return remote(buf.at[g, 1 - y, zz], buf.at[g, 1 - y, zz], sems, (g, zz), (g, zz), to_y())

    for g in range(groups):
        gather_y(qbuf, qy_sem, g, z).start()
        for d in range(1, lines):
            gather_z(qbuf, qz_sem, g, d).start()

    tall = lines * stack
    row_of = lax.rem(lax.broadcasted_iota(jnp.int32, (stack, 1), 0), rows) // steps
    for k in range(2 * lines):
        value = jnp.zeros((stack, 1), jnp.int32)
        for r in range(local_rows):
            value = jnp.where(row_of == r, lens_ref[k * local_rows + r], value)
        lens[k % 2, k // 2 * stack : (k // 2 + 1) * stack] = value

    owner = lax.broadcasted_iota(jnp.int32, (1, span), 1) // page
    within = lax.rem(lax.broadcasted_iota(jnp.int32, (1, span), 1), page)
    place = jnp.zeros((1, span), jnp.int32)
    for j in range(pages):
        place = jnp.where(owner == j, pt_ref[:, j : j + 1], place)
    prow[...] = (seq * pages + place) * page + within
    for g in range(groups):
        k_line = jnp.zeros((1, span), f32)
        v_line = jnp.zeros((1, span), f32)
        for j in range(pages):
            k_line = jnp.where(owner == j, ks_ref[g : g + 1, j : j + 1], k_line)
            v_line = jnp.where(owner == j, vs_ref[g : g + 1, j : j + 1], v_line)
        krow[g] = k_line * inv_root
        vrow[g] = v_line

    def stacked(block):
        return [block[:, j * hd : (j + 1) * hd] for j in range(per)]

    def softmax_terms(scores):
        top = jnp.maximum(jnp.ceil(jnp.max(scores, axis=-1, keepdims=True)), FLOOR)
        terms = jnp.exp2(scores - top)
        total = jnp.sum(terms, axis=-1, keepdims=True)
        lane = lax.broadcasted_iota(jnp.int32, (scores.shape[0], 128), 1)
        return terms, jnp.where(lane == 0, top, total).T[0:2]

    def columns_of(lines_in):
        shape = (128, lines_in[0].shape[1])
        sublane = lax.broadcasted_iota(jnp.int32, shape, 0)
        table = jnp.zeros(shape, f32)
        for i, value in enumerate(lines_in):
            table = jnp.where(sublane == i, value, table)
        table = table.T
        return [table[:, i : i + 1] for i in range(len(lines_in))]

    fkp[...] = jnp.zeros_like(fkp)
    fvp[...] = jnp.zeros_like(fvp)
    fkp[0:rows] = fk_ref[...].reshape(rows, groups * hd)
    fvp[0:rows] = fv_ref[...].reshape(rows, groups * hd)
    slots = fkp.shape[0]
    token = lax.rem(lax.broadcasted_iota(jnp.int32, (stack, slots), 0), rows)
    key_token = lax.broadcasted_iota(jnp.int32, (stack, slots), 1)
    allowed = (token // steps == key_token // steps) & (key_token <= token)
    for g in range(groups):
        at = slice(g * hd, (g + 1) * hd)
        scores = lax.dot_general(
            jnp.concatenate(stacked(qbuf.at[g, y, z]), axis=0),
            fkp[:, at],
            (((1,), (1,)), ((), ())),
            preferred_element_type=f32,
        )
        terms, fstat[g] = softmax_terms(jnp.where(allowed, scores * inv_root, NEG_FILL))
        facc[g] = jnp.dot(terms.astype(bf16), fvp[:, at], preferred_element_type=f32)
    flat_res = res_ref[...].reshape(rows, width)
    for g in range(groups):
        hs[g] = flat_res[:, g * group_width : (g + 1) * group_width].astype(f32)
    gacc[...] = jnp.zeros_like(gacc)

    for copy in cache_copies:
        copy.wait()

    def attend(g, yy):
        heads = [head for zz in range(lines) for head in stacked(qbuf.at[g, yy, zz])]
        scores = lax.dot_general(
            jnp.concatenate(heads, axis=0),
            kbuf[g],
            (((1,), (1,)), ((), ())),
            preferred_element_type=f32,
        )
        scores = jnp.where(prow[...] < lens[yy], scores * krow[g], NEG_FILL)
        terms, stat[g, yy] = softmax_terms(scores)
        part[g, yy] = (
            jnp.dot((terms * vrow[g]).astype(bf16), vbuf[g], preferred_element_type=f32)
            .astype(bf16)
            .reshape(lines, stack, hd)
        )

    def part_y(g):
        src = (part.at[g, 1 - y], stat.at[g, 1 - y])
        dst = (ypart.at[g], ystat.at[g])
        return [remote(src[i], dst[i], py_sem, (i, g), (i, g), to_y()) for i in range(2)]

    def part_z(g, zz, at):
        src, dst = (spart.at[g, zz], sstat.at[g, zz]), (zpart.at[g, at], zstat.at[g, at])
        return [remote(src[i], dst[i], pz_sem, (i, g, zz), (i, g, at), to_z(zz)) for i in range(2)]

    def join(g):
        for copy in part_y(g):
            copy.wait_recv()
        first, second = stat[g, y], ystat[g]
        top = jnp.maximum(first[0:1], second[0:1])
        a, b = jnp.exp2(first[0:1] - top), jnp.exp2(second[0:1] - top)
        total = first[1:2] * a + second[1:2] * b
        for zz in range(lines):
            at = slice(zz * stack, (zz + 1) * stack)
            sstat[g, zz, 0:1] = top[:, at]
            sstat[g, zz, 1:2] = total[:, at]
        a, b = columns_of([a, b])
        joined = (
            part[g, y].reshape(tall, hd).astype(f32) * a
            + ypart[g].reshape(tall, hd).astype(f32) * b
        )
        spart[g] = joined.astype(bf16).reshape(lines, stack, hd)
        for d in range(1, lines):
            for copy in part_z(g, line(d), z):
                copy.start()

    def finish(g):
        others = [line(d) for d in range(1, lines)]
        for zz in others:
            for copy in part_z(g, zz, zz):
                copy.wait_recv()
        mine = pl.ds(pl.multiple_of(z * stack, stack), stack)
        stats = [fstat[g], stat[g, y, :, mine], ystat[g, :, mine]] + [zstat[g, zz] for zz in others]
        parts = [facc[g], part[g, y, z], ypart[g, z]] + [zpart[g, zz] for zz in others]
        top = functools.reduce(jnp.maximum, [s[0:1] for s in stats])
        factors = [jnp.exp2(s[0:1] - top) for s in stats]
        total = sum(s[1:2] * f for s, f in zip(stats, factors))
        factors = columns_of([f / total for f in factors])
        attention = sum(p.astype(f32) * f for p, f in zip(parts, factors))
        square = jnp.zeros((rows, hd), f32)
        for j in range(per):
            at = slice(j * hd, (j + 1) * hd)
            state = hs[g, :, at] + attention[j * rows : (j + 1) * rows]
            hs[g, :, at] = state
            square += state * state
        sq[2 + g] = square
        nbuf[g, y, z] = (hs[g] * gain[g]).astype(bf16)
        gather_y(nbuf, ny_sem, g, z).start()
        for d in range(1, lines):
            gather_z(nbuf, nz_sem, g, d).start()

    def forward(buf, z_sems, y_sems, g):
        for d in range(1, lines):
            gather_z_arrival(buf, z_sems, g, line(d)).wait_recv()
            gather_y(buf, y_sems, g, line(d)).start()

    def arrivals(buf, y_sems, g):
        for d in range(lines):
            gather_y_arrival(buf, y_sems, g, line(d)).wait_recv()

    square_copy = remote(sq.at[0], sq.at[1], sq_sem, (0,), (0,), to_core())

    all_rows = 2 * lines * rows
    tiles = 2 * half // TILE

    def swap(t):
        return remote(gacc.at[0, t], grecv.at[t], g_sem, (t,), (t,), to_core())

    def gate_up(g):
        for slot, at in ((0, 1 - core), (1, core)):
            for t in range(tiles):
                gacc[slot, t] += jnp.dot(
                    nbuf[g].reshape(all_rows, group_width),
                    wgu[
                        at,
                        pl.ds(pl.multiple_of(g * group_width, group_width), group_width),
                        t * TILE : (t + 1) * TILE,
                    ],
                    preferred_element_type=f32,
                )
            if slot == 0:

                @pl.when(g == groups - 1)
                def _():
                    for t in range(tiles):
                        swap(t).start()

    forward(qbuf, qz_sem, qy_sem, 0)

    @pl.loop(0, groups + 4)
    def _(i):
        @pl.when(i < groups)
        def _():
            for p in range(lines):
                for copy in gate_up_copies(i * lines + p):
                    copy.start()

        @pl.when(i >= 4)
        def _():
            for p in range(lines):
                down_copy((i - 4) * lines + p).start()

        @pl.when(i == groups + 3)
        def _():
            forward(ibuf, iz_sem, iy_sem, 0)

        @pl.when(i < groups)
        def _():
            attend(i, y)

        @pl.when(i + 1 < groups)
        def _():
            forward(qbuf, qz_sem, qy_sem, i + 1)

        @pl.when(i < groups)
        def _():
            arrivals(qbuf, qy_sem, i)
            attend(i, 1 - y)
            for copy in part_y(i):
                copy.start()

        @pl.when(i >= 4)
        def _():
            for p in range(lines):
                for copy in gate_up_copies((i - 4) * lines + p):
                    copy.wait()
            arrivals(nbuf, ny_sem, i - 4)
            gate_up(i - 4)

        @pl.when((i >= 3) & (i < groups + 3))
        def _():
            forward(nbuf, nz_sem, ny_sem, i - 3)

        @pl.when(i == groups + 2)
        def _():
            square_copy.wait_recv()
            inverse = lax.rsqrt((sq[0] + sq[1]) / (2 * width) + EPSILON)
            ibuf[0, y, z] = inverse
            gather_y(ibuf, iy_sem, 0, z).start()
            for d in range(1, lines):
                gather_z(ibuf, iz_sem, 0, d).start()

        @pl.when((i >= 1) & (i < groups + 1))
        def _():
            join(i - 1)

        @pl.when((i >= 2) & (i < groups + 2))
        def _():
            finish(i - 2)

        @pl.when(i == groups + 1)
        def _():
            square = sum(sq[2 + g] for g in range(groups))
            sq[0] = jnp.broadcast_to(jnp.sum(square, axis=-1, keepdims=True), (rows, 128))
            square_copy.start()

    arrivals(ibuf, iy_sem, 0)
    for t in range(tiles):
        swap(t).wait_recv()
    for b in range(half // 128):
        inverse = ibuf[0].reshape(all_rows, 128)

        def summed(column):
            t, at = column // TILE, slice(column % TILE, column % TILE + 128)
            return (gacc[1, t, :, at] + grecv[t, :, at]) * inverse

        gate, up = summed(b * 128), summed(half + b * 128)
        hbuf[:, pl.ds(pl.multiple_of(core * half + b * 128, 128), 128)] = (
            gate / (1.0 + jnp.exp(-gate)) * up
        ).astype(bf16)

    def hidden_copy(at):
        both = hbuf.at[:, pl.ds(pl.multiple_of(at * half, 128), half)]
        return remote(both, both, h_sem, (0,), (0,), to_core())

    hidden_copy(core).start()

    @pl.loop(0, pairs)
    def _(p):
        down_copy(p).wait()

    hidden_copy(1 - core).wait_recv()

    chunk = width // CHUNKS

    def down_y(c):
        return remote(dpart.at[c], dy.at[c], dy_sem, (c,), (c,), to_y())

    def down_z(c, zz, at):
        return remote(dsum.at[c, zz], dz.at[c, at], dz_sem, (c, zz), (c, at), to_z(zz))

    def relay(c):
        down_y(c).wait_recv()
        for d in range(1, lines):
            zz = line(d)
            dsum[c, zz] = (dacc[c, y, zz] + dy[c, zz].astype(f32)).astype(bf16)
            down_z(c, zz, z).start()

    @pl.loop(0, CHUNKS)
    def _(c):
        for t in range(chunk // TILE):
            dacc[c, :, :, :, t * TILE : (t + 1) * TILE] = jnp.dot(
                hbuf[...],
                wd[:, pl.ds(pl.multiple_of(c * chunk + t * TILE, TILE), TILE)],
                preferred_element_type=f32,
            ).reshape(2, lines, rows, TILE)
        dpart[c] = dacc[c, 1 - y].astype(bf16)
        down_y(c).start()

        @pl.when(c >= LAG)
        def _():
            relay(c - LAG)

    for c in range(CHUNKS - LAG, CHUNKS):
        relay(c)
    for c in range(CHUNKS):
        g, first = c * chunk // group_width, c * chunk % group_width
        value = hs[g, :, first : first + chunk] + dacc[c, y, z] + dy[c, z].astype(f32)
        for d in range(1, lines):
            down_z(c, line(d), line(d)).wait_recv()
            value += dz[c, line(d)].astype(f32)
        out_ref[:, :, c * chunk : (c + 1) * chunk] = value.astype(out_ref.dtype).reshape(
            local_rows, steps, chunk
        )

    @pl.loop(0, groups)
    def _(g):
        for d in range(1, lines):
            gather_z(qbuf, qz_sem, g, d).wait_send()
            gather_z(nbuf, nz_sem, g, d).wait_send()
            for copy in part_z(g, line(d), z):
                copy.wait_send()
        for d in range(lines):
            gather_y(qbuf, qy_sem, g, line(d)).wait_send()
            gather_y(nbuf, ny_sem, g, line(d)).wait_send()
        for copy in part_y(g):
            copy.wait_send()

    @pl.loop(0, CHUNKS)
    def _(c):
        down_y(c).wait_send()
        for d in range(1, lines):
            down_z(c, line(d), z).wait_send()

    for t in range(tiles):
        swap(t).wait_send()
    for d in range(1, lines):
        gather_z(ibuf, iz_sem, 0, d).wait_send()
    for d in range(lines):
        gather_y(ibuf, iy_sem, 0, line(d)).wait_send()
    square_copy.wait_send()
    hidden_copy(core).wait_send()


def kernel_body(
    lines,
    queries,
    fresh_keys,
    fresh_values,
    residual_in,
    cache_keys,
    cache_values,
    key_scales,
    value_scales,
    page_table,
    row_lengths,
    norm_gain,
    w_gate,
    w_up,
    w_down,
):
    local_rows, steps, width = queries.shape
    groups, span, hd = cache_keys.shape
    rows = local_rows * steps
    group_width = width // groups
    stack = rows * group_width // hd
    fresh_width = fresh_keys.shape[2]
    hidden = w_gate.shape[1]
    half = hidden // 2
    tiles = hidden // TILE
    chunk = width // CHUNKS
    all_rows = 2 * lines * rows
    bf16, f32 = jnp.bfloat16, jnp.float32
    vmem = pl.BlockSpec(memory_space=pltpu.VMEM)
    smem = pl.BlockSpec(memory_space=pltpu.SMEM)
    anywhere = pl.BlockSpec(memory_space=pl.ANY)
    dma = pltpu.SemaphoreType.DMA
    return pl.pallas_call(
        functools.partial(layer_kernel, lines),
        out_shape=jax.ShapeDtypeStruct(queries.shape, bf16),
        in_specs=[vmem] * 4 + [smem] + [vmem] * 4 + [anywhere] * 5,
        out_specs=vmem,
        scratch_shapes=[
            pltpu.VMEM((groups, span, hd), bf16),
            pltpu.VMEM((groups, span, hd), bf16),
            pltpu.VMEM((2, width, 2 * half), bf16),
            pltpu.VMEM(w_down.shape, bf16),
            pltpu.VMEM((groups, 2, lines, rows, group_width), bf16),
            pltpu.VMEM((2, lines * stack, 1), jnp.int32),
            pltpu.VMEM((groups, 1, span), f32),
            pltpu.VMEM((groups, 1, span), f32),
            pltpu.VMEM((1, span), jnp.int32),
            pltpu.VMEM((128, fresh_width), bf16),
            pltpu.VMEM((128, fresh_width), bf16),
            pltpu.VMEM((groups, stack, hd), f32),
            pltpu.VMEM((groups, 2, stack), f32),
            pltpu.VMEM((groups, 2, lines, stack, hd), bf16),
            pltpu.VMEM((groups, 2, 2, lines * stack), f32),
            pltpu.VMEM((groups, lines, stack, hd), bf16),
            pltpu.VMEM((groups, 2, lines * stack), f32),
            pltpu.VMEM((groups, lines, stack, hd), bf16),
            pltpu.VMEM((groups, lines, 2, stack), f32),
            pltpu.VMEM((groups, lines, stack, hd), bf16),
            pltpu.VMEM((groups, lines, 2, stack), f32),
            pltpu.VMEM((groups, rows, group_width), f32),
            pltpu.VMEM((2 + groups, rows, 128), f32),
            pltpu.VMEM((1, 2, lines, rows, 128), f32),
            pltpu.VMEM((groups, 2, lines, rows, group_width), bf16),
            pltpu.VMEM((2, tiles, all_rows, TILE), f32),
            pltpu.VMEM((tiles, all_rows, TILE), f32),
            pltpu.VMEM((all_rows, hidden), bf16),
            pltpu.VMEM((CHUNKS, 2, lines, rows, chunk), f32),
            pltpu.VMEM((CHUNKS, lines, rows, chunk), bf16),
            pltpu.VMEM((CHUNKS, lines, rows, chunk), bf16),
            pltpu.VMEM((CHUNKS, lines, rows, chunk), bf16),
            pltpu.VMEM((CHUNKS, lines, rows, chunk), bf16),
            dma((2,)),
            dma((5, groups * lines)),
            dma((2, groups, lines)),
            dma((2, groups, lines)),
            dma((2, 2, groups)),
            dma((2, 2, groups, lines)),
            dma((2, 1)),
            dma((2, 1, lines)),
            dma((2, 1, lines)),
            dma((2, groups, lines)),
            dma((2, groups, lines)),
            dma((2, tiles)),
            dma((2, 1)),
            dma((2, CHUNKS)),
            dma((2, CHUNKS, lines)),
        ],
        compiler_params=pltpu.CompilerParams(
            collective_id=0, has_side_effects=True, vmem_limit_bytes=62 * 1024 * 1024
        ),
    )(
        queries,
        fresh_keys,
        fresh_values,
        residual_in,
        row_lengths,
        key_scales,
        value_scales,
        page_table,
        norm_gain.reshape(groups, 1, group_width),
        cache_keys,
        cache_values,
        w_gate,
        w_up,
        w_down,
    )


def choose_body(seq_size, cores, *args):
    local_rows, steps, width = args[0].shape
    groups, _, head_dim = args[4].shape
    rows, hidden = local_rows * steps, args[11].shape[1]
    stack = rows * width // (groups * head_dim)
    pairs = groups * (seq_size // 2)
    weights = 2 * 3 * width * hidden
    fits = (
        cores == 2
        and seq_size % 2 == 0
        and rows % 16 == 0
        and stack == 128
        and head_dim == 128
        and hidden % 256 == 0
        and hidden % (16 * pairs) == 0
        and width % (16 * pairs) == 0
        and width % (CHUNKS * TILE) == 0
        and CHUNKS % groups == 0
        and weights <= 44 * 1024 * 1024
    )
    if fits:
        return kernel_body(seq_size // 2, *args)
    return plain_body(*args)


def solution(mesh):
    in_specs = (
        P(("groups", "seq"), None, "tensor"),
        P(("groups", "seq"), None, "tensor"),
        P(("groups", "seq"), None, "tensor"),
        P(("groups", "seq"), None, "tensor"),
        P("tensor", ("groups", "seq"), None),
        P("tensor", ("groups", "seq"), None),
        P("tensor", ("groups", "seq")),
        P("tensor", ("groups", "seq")),
        P(("groups", "seq"), None),
        P("groups"),
        P("tensor"),
        P("tensor", "seq"),
        P("tensor", "seq"),
        P("seq", "tensor"),
    )
    out_specs = P(("groups", "seq"), None, "tensor")
    body = functools.partial(choose_body, mesh.shape["seq"], mesh.shape["tensor"])
    return jax.shard_map(body, mesh=mesh, in_specs=in_specs, out_specs=out_specs, check_vma=False)
```

```python
import functools
import math

import jax
import jax.numpy as jnp
from jax import lax
from jax.experimental import pallas as pl
from jax.experimental.pallas import tpu as pltpu
from jax.sharding import PartitionSpec as P

D = 8192


NEG_FILL = -1e30
EPSILON = 1e-05
LOG2E = 1.4426950408889634


def combine_partials(earlier, later):
    shared_top = jnp.maximum(earlier[0], later[0])
    early_factor = jnp.exp2(earlier[0] - shared_top)
    late_factor = jnp.exp2(later[0] - shared_top)
    return (
        shared_top,
        earlier[1] * early_factor + later[1] * late_factor,
        earlier[2] * early_factor[..., None] + later[2] * late_factor[..., None],
    )


def masked_terms(scores, allowed_mask):
    row_top = jnp.ceil(jnp.max(jnp.where(allowed_mask, scores, NEG_FILL), axis=-1))
    exp_terms = jnp.where(allowed_mask, jnp.exp2(scores - row_top[..., None]), 0.0)
    return (row_top, exp_terms)


def plain_body(
    queries,
    fresh_keys,
    fresh_values,
    residual_in,
    cache_keys,
    cache_values,
    key_scales,
    value_scales,
    page_table,
    row_lengths,
    norm_gain,
    w_gate,
    w_up,
    w_down,
):
    local_rows = queries.shape[0]
    step_count = queries.shape[1]
    half_width = queries.shape[2]
    groups = cache_keys.shape[0]
    cache_span = cache_keys.shape[1]
    head_dim = cache_keys.shape[2]
    page_count = page_table.shape[1]
    block_size = cache_span // page_count
    heads_per = half_width // (groups * head_dim)
    inv_root = LOG2E / math.sqrt(head_dim)
    seq_index = lax.axis_index("seq")
    all_q, all_fk, all_fv, all_x = (
        lax.all_gather(queries, "seq", axis=0, tiled=True),
        lax.all_gather(fresh_keys, "seq", axis=0, tiled=True),
        lax.all_gather(fresh_values, "seq", axis=0, tiled=True),
        lax.all_gather(residual_in, "seq", axis=0, tiled=True),
    )
    all_rows = all_q.shape[0]
    offsets = jnp.arange(cache_span, dtype=jnp.int32)
    logical = seq_index * page_count + jnp.repeat(page_table[0], block_size)
    position = logical * block_size + offsets % block_size
    visible = position[None, :] < row_lengths[:, None]
    k_scale = jnp.repeat(key_scales, block_size, axis=1)
    v_scale = jnp.repeat(value_scales, block_size, axis=1)
    q_part = all_q.reshape(all_rows, step_count, groups, heads_per, head_dim)
    q_part = jnp.moveaxis(q_part, 2, 0)

    def per_group(operands):
        q_group, key_block, value_block, k_row, v_row = operands
        raw_scores = jnp.einsum(
            "nsqd,cd->nsqc", q_group, key_block, preferred_element_type=jnp.float32
        )
        scores = raw_scores * k_row * inv_root
        row_top, exp_terms = masked_terms(scores, visible[:, None, None, :])
        row_total = jnp.sum(exp_terms, axis=-1)
        weights = (exp_terms * v_row).astype(jnp.bfloat16)
        weighted = jnp.einsum(
            "nsqc,cd->nsqd", weights, value_block, preferred_element_type=jnp.float32
        )
        return (row_top, row_total, weighted)

    partial_value = lax.map(per_group, (q_part, cache_keys, cache_values, k_scale, v_scale))
    row_peak = lax.pmax(partial_value[0], "seq")
    factor = jnp.exp2(partial_value[0] - row_peak)
    row_total, weighted = lax.psum(
        (partial_value[1] * factor, partial_value[2] * factor[..., None]), "seq"
    )
    row_count = all_q.shape[0]
    fresh_row_count = all_q.shape[0]
    q_part = all_q.reshape(fresh_row_count, step_count, groups, heads_per, head_dim)
    k_part = all_fk.reshape(fresh_row_count, step_count, groups, head_dim)
    v_part = all_fv.reshape(fresh_row_count, step_count, groups, head_dim)
    raw_scores = jnp.einsum("nsgqd,ntgd->gnsqt", q_part, k_part, preferred_element_type=jnp.float32)
    scores = raw_scores * inv_root
    allowed = jnp.arange(step_count)[None, :] <= (0 + jnp.arange(step_count))[:, None]
    row_top, exp_terms = masked_terms(scores, allowed[None, None, :, None, :])
    fresh_row_total = jnp.sum(exp_terms, axis=-1)
    fresh_weighted = jnp.einsum(
        "gnsqt,ntgd->gnsqd",
        exp_terms.astype(jnp.bfloat16),
        v_part,
        preferred_element_type=jnp.float32,
    )
    joined = combine_partials(
        (row_peak, row_total, weighted), (row_top, fresh_row_total, fresh_weighted)
    )
    attention = joined[2] / joined[1][..., None]
    attention = jnp.moveaxis(attention, 0, 2).reshape(row_count, step_count, half_width)
    hidden_state = all_x.astype(jnp.float32) + attention
    square = lax.psum(jnp.sum(hidden_state * hidden_state, axis=-1), "tensor")
    inverse_rms = lax.rsqrt(square / D + EPSILON)
    normed = (hidden_state * inverse_rms[..., None] * norm_gain).astype(jnp.bfloat16)
    hidden_state, normed = (hidden_state, normed)
    own_state = lax.dynamic_slice_in_dim(hidden_state, seq_index * local_rows, local_rows, 0)
    flat_normed = normed.reshape(all_rows * step_count, half_width)
    gate_part = jnp.dot(flat_normed, w_gate, preferred_element_type=jnp.float32)
    up_part = jnp.dot(flat_normed, w_up, preferred_element_type=jnp.float32)
    gate_sums, up_sums = lax.psum((gate_part, up_part), "tensor")
    hidden = (jax.nn.silu(gate_sums) * up_sums).astype(jnp.bfloat16)
    down_sums = lax.psum_scatter(
        jnp.dot(hidden, w_down, preferred_element_type=jnp.float32),
        "seq",
        scatter_dimension=0,
        tiled=True,
    )
    return (own_state + down_sums.reshape(local_rows, step_count, half_width)).astype(jnp.bfloat16)


MESH = pl.DeviceIdType.MESH
FLOOR = -1e29
CHUNKS = 8
TILE = 256
LAG = 3
WIDE = 4


def layer_kernel(
    lines,
    q_ref,
    fk_ref,
    fv_ref,
    res_ref,
    lens_ref,
    ks_ref,
    vs_ref,
    pt_ref,
    gain,
    ck_hbm,
    cv_hbm,
    wg_hbm,
    wu_hbm,
    wd_hbm,
    out_ref,
    kbuf,
    vbuf,
    wgu,
    wd,
    qbuf,
    lens,
    krow,
    vrow,
    prow,
    fkp,
    fvp,
    facc,
    fstat,
    part,
    stat,
    ypart,
    ystat,
    spart,
    sstat,
    zpart,
    zstat,
    hs,
    sq,
    ibuf,
    nbuf,
    gacc,
    grecv,
    hbuf,
    dacc,
    dpart,
    dy,
    dsum,
    dz,
    local_sem,
    w_sem,
    qz_sem,
    qy_sem,
    py_sem,
    pz_sem,
    sq_sem,
    iz_sem,
    iy_sem,
    nz_sem,
    ny_sem,
    g_sem,
    h_sem,
    dy_sem,
    dz_sem,
):
    f32 = jnp.float32
    bf16 = jnp.bfloat16
    seq = lax.axis_index("seq")
    core = lax.axis_index("tensor")
    z, y = seq // 2, lax.rem(seq, 2)
    groups, span, hd = kbuf.shape
    local_rows, steps, width = q_ref.shape
    rows = local_rows * steps
    group_width = width // groups
    per = group_width // hd
    stack = per * rows
    pages = pt_ref.shape[1]
    page = span // pages
    inv_root = LOG2E / math.sqrt(hd)
    half = hbuf.shape[1] // 2

    def line(d):
        return lax.rem(z + d, lines)

    def to_y():
        return {"seq": z * 2 + 1 - y}

    def to_z(zz):
        return {"seq": zz * 2 + y}

    def to_core():
        return {"tensor": 1 - core}

    def remote(src, dst, sems, send_at, recv_at, where):
        return pltpu.make_async_remote_copy(
            src_ref=src,
            dst_ref=dst,
            send_sem=sems.at[(0,) + send_at],
            recv_sem=sems.at[(1,) + recv_at],
            device_id=where,
            device_id_type=MESH,
        )

    cache_copies = [
        pltpu.make_async_copy(ck_hbm, kbuf, local_sem.at[0]),
        pltpu.make_async_copy(cv_hbm, vbuf, local_sem.at[1]),
    ]

    def gate_up_copies(p):
        piece = width // groups
        at = pl.ds(pl.multiple_of(p * piece, 16), piece)
        return [
            pltpu.make_async_copy(
                src.at[at, pl.ds(h * half, half)],
                wgu.at[h, at, pl.ds(i * half, half)],
                w_sem.at[2 * i + h, p],
            )
            for i, src in enumerate((wg_hbm, wu_hbm))
            for h in range(2)
        ]

    def down_copy(p):
        piece = wd_hbm.shape[0] // groups
        at = pl.ds(pl.multiple_of(p * piece, 16), piece)
        return pltpu.make_async_copy(wd_hbm.at[at], wd.at[at], w_sem.at[4, p])

    for copy in cache_copies:
        copy.start()

    barrier = pltpu.get_barrier_semaphore()
    peers = [to_y(), to_core()] + [to_z(line(d)) for d in range(1, lines)]
    for where in peers:
        pl.semaphore_signal(barrier, inc=1, device_id=where, device_id_type=MESH)

    flat_q = q_ref[...].reshape(rows, width)
    for g in range(groups):
        qbuf[g, y, z] = flat_q[:, g * group_width : (g + 1) * group_width]
    pl.semaphore_wait(barrier, len(peers))

    def gather_z(buf, sems, g, d):
        return remote(buf.at[g, y, z], buf.at[g, y, z], sems, (g, d), (g, z), to_z(line(d)))

    def gather_z_arrival(buf, sems, g, zz):
        return remote(buf.at[g, y, zz], buf.at[g, y, zz], sems, (g, 0), (g, zz), to_z(zz))

    def gather_y(buf, sems, g, zz):
        return remote(buf.at[g, y, zz], buf.at[g, y, zz], sems, (g, zz), (g, zz), to_y())

    def gather_y_arrival(buf, sems, g, zz):
        return remote(buf.at[g, 1 - y, zz], buf.at[g, 1 - y, zz], sems, (g, zz), (g, zz), to_y())

    for g in range(groups):
        gather_y(qbuf, qy_sem, g, z).start()
        for d in range(1, lines):
            gather_z(qbuf, qz_sem, g, d).start()

    tall = lines * stack
    row_of = lax.rem(lax.broadcasted_iota(jnp.int32, (stack, 1), 0), rows) // steps
    for k in range(2 * lines):
        value = jnp.zeros((stack, 1), jnp.int32)
        for r in range(local_rows):
            value = jnp.where(row_of == r, lens_ref[k * local_rows + r], value)
        lens[k % 2, k // 2 * stack : (k // 2 + 1) * stack] = value

    owner = lax.broadcasted_iota(jnp.int32, (1, span), 1) // page
    within = lax.rem(lax.broadcasted_iota(jnp.int32, (1, span), 1), page)
    place = jnp.zeros((1, span), jnp.int32)
    for j in range(pages):
        place = jnp.where(owner == j, pt_ref[:, j : j + 1], place)
    prow[...] = (seq * pages + place) * page + within
    for g in range(groups):
        k_line = jnp.zeros((1, span), f32)
        v_line = jnp.zeros((1, span), f32)
        for j in range(pages):
            k_line = jnp.where(owner == j, ks_ref[g : g + 1, j : j + 1], k_line)
            v_line = jnp.where(owner == j, vs_ref[g : g + 1, j : j + 1], v_line)
        krow[g] = k_line * inv_root
        vrow[g] = v_line

    def stacked(block):
        return [block[:, j * hd : (j + 1) * hd] for j in range(per)]

    def softmax_terms(scores):
        top = jnp.maximum(jnp.ceil(jnp.max(scores, axis=-1, keepdims=True)), FLOOR)
        terms = jnp.exp2(scores - top)
        total = jnp.sum(terms, axis=-1, keepdims=True)
        lane = lax.broadcasted_iota(jnp.int32, (scores.shape[0], 128), 1)
        return terms, jnp.where(lane == 0, top, total).T[0:2]

    def columns_of(lines_in):
        shape = (128, lines_in[0].shape[1])
        sublane = lax.broadcasted_iota(jnp.int32, shape, 0)
        table = jnp.zeros(shape, f32)
        for i, value in enumerate(lines_in):
            table = jnp.where(sublane == i, value, table)
        table = table.T
        return [table[:, i : i + 1] for i in range(len(lines_in))]

    fkp[...] = jnp.zeros_like(fkp)
    fvp[...] = jnp.zeros_like(fvp)
    fkp[0:rows] = fk_ref[...].reshape(rows, groups * hd)
    fvp[0:rows] = fv_ref[...].reshape(rows, groups * hd)
    slots = fkp.shape[0]
    token = lax.rem(lax.broadcasted_iota(jnp.int32, (stack, slots), 0), rows)
    key_token = lax.broadcasted_iota(jnp.int32, (stack, slots), 1)
    allowed = (token // steps == key_token // steps) & (key_token <= token)
    for g in range(groups):
        at = slice(g * hd, (g + 1) * hd)
        scores = lax.dot_general(
            jnp.concatenate(stacked(qbuf.at[g, y, z]), axis=0),
            fkp[:, at],
            (((1,), (1,)), ((), ())),
            preferred_element_type=f32,
        )
        terms, fstat[g] = softmax_terms(jnp.where(allowed, scores * inv_root, NEG_FILL))
        facc[g] = jnp.dot(terms.astype(bf16), fvp[:, at], preferred_element_type=f32)
    flat_res = res_ref[...].reshape(rows, width)
    for g in range(groups):
        hs[g] = flat_res[:, g * group_width : (g + 1) * group_width].astype(f32)
    gacc[...] = jnp.zeros_like(gacc)

    for copy in cache_copies:
        copy.wait()

    def attend(g, yy):
        heads = [head for zz in range(lines) for head in stacked(qbuf.at[g, yy, zz])]
        scores = lax.dot_general(
            jnp.concatenate(heads, axis=0),
            kbuf[g],
            (((1,), (1,)), ((), ())),
            preferred_element_type=f32,
        )
        scores = jnp.where(prow[...] < lens[yy], scores * krow[g], NEG_FILL)
        terms, stat[g, yy] = softmax_terms(scores)
        part[g, yy] = (
            jnp.dot((terms * vrow[g]).astype(bf16), vbuf[g], preferred_element_type=f32)
            .astype(bf16)
            .reshape(lines, stack, hd)
        )

    def part_y(g):
        src = (part.at[g, 1 - y], stat.at[g, 1 - y])
        dst = (ypart.at[g], ystat.at[g])
        return [remote(src[i], dst[i], py_sem, (i, g), (i, g), to_y()) for i in range(2)]

    def part_z(g, zz, at):
        src, dst = (spart.at[g, zz], sstat.at[g, zz]), (zpart.at[g, at], zstat.at[g, at])
        return [remote(src[i], dst[i], pz_sem, (i, g, zz), (i, g, at), to_z(zz)) for i in range(2)]

    def join(g):
        for copy in part_y(g):
            copy.wait_recv()
        first, second = stat[g, y], ystat[g]
        top = jnp.maximum(first[0:1], second[0:1])
        a, b = jnp.exp2(first[0:1] - top), jnp.exp2(second[0:1] - top)
        total = first[1:2] * a + second[1:2] * b
        for zz in range(lines):
            at = slice(zz * stack, (zz + 1) * stack)
            sstat[g, zz, 0:1] = top[:, at]
            sstat[g, zz, 1:2] = total[:, at]
        a, b = columns_of([a, b])
        joined = (
            part[g, y].reshape(tall, hd).astype(f32) * a
            + ypart[g].reshape(tall, hd).astype(f32) * b
        )
        spart[g] = joined.astype(bf16).reshape(lines, stack, hd)
        for d in range(1, lines):
            for copy in part_z(g, line(d), z):
                copy.start()

    def finish(g):
        others = [line(d) for d in range(1, lines)]
        for zz in others:
            for copy in part_z(g, zz, zz):
                copy.wait_recv()
        mine = pl.ds(pl.multiple_of(z * stack, stack), stack)
        stats = [fstat[g], stat[g, y, :, mine], ystat[g, :, mine]] + [zstat[g, zz] for zz in others]
        parts = [facc[g], part[g, y, z], ypart[g, z]] + [zpart[g, zz] for zz in others]
        top = functools.reduce(jnp.maximum, [s[0:1] for s in stats])
        factors = [jnp.exp2(s[0:1] - top) for s in stats]
        total = sum(s[1:2] * f for s, f in zip(stats, factors))
        factors = columns_of([f / total for f in factors])
        attention = sum(p.astype(f32) * f for p, f in zip(parts, factors))
        square = jnp.zeros((rows, hd), f32)
        for j in range(per):
            at = slice(j * hd, (j + 1) * hd)
            state = hs[g, :, at] + attention[j * rows : (j + 1) * rows]
            hs[g, :, at] = state
            square += state * state
        sq[2 + g] = square
        nbuf[g, y, z] = (hs[g] * gain[g]).astype(bf16)
        gather_y(nbuf, ny_sem, g, z).start()
        for d in range(1, lines):
            gather_z(nbuf, nz_sem, g, d).start()

    def forward(buf, z_sems, y_sems, g):
        for d in range(1, lines):
            gather_z_arrival(buf, z_sems, g, line(d)).wait_recv()
            gather_y(buf, y_sems, g, line(d)).start()

    def arrivals(buf, y_sems, g):
        for d in range(lines):
            gather_y_arrival(buf, y_sems, g, line(d)).wait_recv()

    square_copy = remote(sq.at[0], sq.at[1], sq_sem, (0,), (0,), to_core())

    all_rows = 2 * lines * rows
    tiles = 2 * half // TILE

    def swap(t):
        return remote(gacc.at[0, t], grecv.at[t], g_sem, (t,), (t,), to_core())

    def gate_up(g):
        for slot, at in ((0, 1 - core), (1, core)):
            for first in range(0, tiles, WIDE):
                last = min(first + WIDE, tiles)
                product = jnp.dot(
                    nbuf[g].reshape(all_rows, group_width),
                    wgu[
                        at,
                        pl.ds(pl.multiple_of(g * group_width, group_width), group_width),
                        first * TILE : last * TILE,
                    ],
                    preferred_element_type=f32,
                )
                for t in range(first, last):
                    gacc[slot, t] += product[:, (t - first) * TILE : (t - first + 1) * TILE]
            if slot == 0:

                @pl.when(g == groups - 1)
                def _():
                    for t in range(tiles):
                        swap(t).start()

    forward(qbuf, qz_sem, qy_sem, 0)

    @pl.loop(0, groups + 4)
    def _(i):
        @pl.when(i < groups)
        def _():
            for copy in gate_up_copies(i):
                copy.start()

        @pl.when(i >= 4)
        def _():
            down_copy(i - 4).start()

        @pl.when(i == groups + 3)
        def _():
            forward(ibuf, iz_sem, iy_sem, 0)

        @pl.when(i < groups)
        def _():
            attend(i, y)

        @pl.when(i + 1 < groups)
        def _():
            forward(qbuf, qz_sem, qy_sem, i + 1)

        @pl.when(i < groups)
        def _():
            arrivals(qbuf, qy_sem, i)
            attend(i, 1 - y)
            for copy in part_y(i):
                copy.start()

        @pl.when(i >= 4)
        def _():
            for copy in gate_up_copies(i - 4):
                copy.wait()
            arrivals(nbuf, ny_sem, i - 4)
            gate_up(i - 4)

        @pl.when((i >= 3) & (i < groups + 3))
        def _():
            forward(nbuf, nz_sem, ny_sem, i - 3)

        @pl.when(i == groups + 2)
        def _():
            square_copy.wait_recv()
            inverse = lax.rsqrt((sq[0] + sq[1]) / (2 * width) + EPSILON)
            ibuf[0, y, z] = inverse
            gather_y(ibuf, iy_sem, 0, z).start()
            for d in range(1, lines):
                gather_z(ibuf, iz_sem, 0, d).start()

        @pl.when((i >= 1) & (i < groups + 1))
        def _():
            join(i - 1)

        @pl.when((i >= 2) & (i < groups + 2))
        def _():
            finish(i - 2)

        @pl.when(i == groups + 1)
        def _():
            square = sum(sq[2 + g] for g in range(groups))
            sq[0] = jnp.broadcast_to(jnp.sum(square, axis=-1, keepdims=True), (rows, 128))
            square_copy.start()

    arrivals(ibuf, iy_sem, 0)
    for t in range(tiles):
        swap(t).wait_recv()
    for b in range(half // 128):
        inverse = ibuf[0].reshape(all_rows, 128)

        def summed(column):
            t, at = column // TILE, slice(column % TILE, column % TILE + 128)
            return (gacc[1, t, :, at] + grecv[t, :, at]) * inverse

        gate, up = summed(b * 128), summed(half + b * 128)
        hbuf[:, pl.ds(pl.multiple_of(core * half + b * 128, 128), 128)] = (
            gate / (1.0 + jnp.exp(-gate)) * up
        ).astype(bf16)

    def hidden_copy(at):
        both = hbuf.at[:, pl.ds(pl.multiple_of(at * half, 128), half)]
        return remote(both, both, h_sem, (0,), (0,), to_core())

    hidden_copy(core).start()

    @pl.loop(0, groups)
    def _(p):
        down_copy(p).wait()

    hidden_copy(1 - core).wait_recv()

    chunk = width // CHUNKS

    def down_y(c):
        return remote(dpart.at[c], dy.at[c], dy_sem, (c,), (c,), to_y())

    def down_z(c, zz, at):
        return remote(dsum.at[c, zz], dz.at[c, at], dz_sem, (c, zz), (c, at), to_z(zz))

    def relay(c):
        down_y(c).wait_recv()
        for d in range(1, lines):
            zz = line(d)
            dsum[c, zz] = (dacc[c, y, zz] + dy[c, zz].astype(f32)).astype(bf16)
            down_z(c, zz, z).start()

    @pl.loop(0, CHUNKS)
    def _(c):
        dacc[c] = jnp.dot(
            hbuf[...],
            wd[:, pl.ds(pl.multiple_of(c * chunk, TILE), chunk)],
            preferred_element_type=f32,
        ).reshape(2, lines, rows, chunk)
        dpart[c] = dacc[c, 1 - y].astype(bf16)
        down_y(c).start()

        @pl.when(c >= LAG)
        def _():
            relay(c - LAG)

    for c in range(CHUNKS - LAG, CHUNKS):
        relay(c)
    for c in range(CHUNKS):
        g, first = c * chunk // group_width, c * chunk % group_width
        value = hs[g, :, first : first + chunk] + dacc[c, y, z] + dy[c, z].astype(f32)
        for d in range(1, lines):
            down_z(c, line(d), line(d)).wait_recv()
            value += dz[c, line(d)].astype(f32)
        out_ref[:, :, c * chunk : (c + 1) * chunk] = value.astype(out_ref.dtype).reshape(
            local_rows, steps, chunk
        )

    @pl.loop(0, groups)
    def _(g):
        for d in range(1, lines):
            gather_z(qbuf, qz_sem, g, d).wait_send()
            gather_z(nbuf, nz_sem, g, d).wait_send()
            for copy in part_z(g, line(d), z):
                copy.wait_send()
        for d in range(lines):
            gather_y(qbuf, qy_sem, g, line(d)).wait_send()
            gather_y(nbuf, ny_sem, g, line(d)).wait_send()
        for copy in part_y(g):
            copy.wait_send()

    @pl.loop(0, CHUNKS)
    def _(c):
        down_y(c).wait_send()
        for d in range(1, lines):
            down_z(c, line(d), z).wait_send()

    for t in range(tiles):
        swap(t).wait_send()
    for d in range(1, lines):
        gather_z(ibuf, iz_sem, 0, d).wait_send()
    for d in range(lines):
        gather_y(ibuf, iy_sem, 0, line(d)).wait_send()
    square_copy.wait_send()
    hidden_copy(core).wait_send()


def kernel_body(
    lines,
    queries,
    fresh_keys,
    fresh_values,
    residual_in,
    cache_keys,
    cache_values,
    key_scales,
    value_scales,
    page_table,
    row_lengths,
    norm_gain,
    w_gate,
    w_up,
    w_down,
):
    local_rows, steps, width = queries.shape
    groups, span, hd = cache_keys.shape
    rows = local_rows * steps
    group_width = width // groups
    stack = rows * group_width // hd
    fresh_width = fresh_keys.shape[2]
    hidden = w_gate.shape[1]
    half = hidden // 2
    tiles = hidden // TILE
    chunk = width // CHUNKS
    all_rows = 2 * lines * rows
    bf16, f32 = jnp.bfloat16, jnp.float32
    vmem = pl.BlockSpec(memory_space=pltpu.VMEM)
    smem = pl.BlockSpec(memory_space=pltpu.SMEM)
    anywhere = pl.BlockSpec(memory_space=pl.ANY)
    dma = pltpu.SemaphoreType.DMA
    return pl.pallas_call(
        functools.partial(layer_kernel, lines),
        out_shape=jax.ShapeDtypeStruct(queries.shape, bf16),
        in_specs=[vmem] * 4 + [smem] + [vmem] * 4 + [anywhere] * 5,
        out_specs=vmem,
        scratch_shapes=[
            pltpu.VMEM((groups, span, hd), bf16),
            pltpu.VMEM((groups, span, hd), bf16),
            pltpu.VMEM((2, width, 2 * half), bf16),
            pltpu.VMEM(w_down.shape, bf16),
            pltpu.VMEM((groups, 2, lines, rows, group_width), bf16),
            pltpu.VMEM((2, lines * stack, 1), jnp.int32),
            pltpu.VMEM((groups, 1, span), f32),
            pltpu.VMEM((groups, 1, span), f32),
            pltpu.VMEM((1, span), jnp.int32),
            pltpu.VMEM((128, fresh_width), bf16),
            pltpu.VMEM((128, fresh_width), bf16),
            pltpu.VMEM((groups, stack, hd), f32),
            pltpu.VMEM((groups, 2, stack), f32),
            pltpu.VMEM((groups, 2, lines, stack, hd), bf16),
            pltpu.VMEM((groups, 2, 2, lines * stack), f32),
            pltpu.VMEM((groups, lines, stack, hd), bf16),
            pltpu.VMEM((groups, 2, lines * stack), f32),
            pltpu.VMEM((groups, lines, stack, hd), bf16),
            pltpu.VMEM((groups, lines, 2, stack), f32),
            pltpu.VMEM((groups, lines, stack, hd), bf16),
            pltpu.VMEM((groups, lines, 2, stack), f32),
            pltpu.VMEM((groups, rows, group_width), f32),
            pltpu.VMEM((2 + groups, rows, 128), f32),
            pltpu.VMEM((1, 2, lines, rows, 128), f32),
            pltpu.VMEM((groups, 2, lines, rows, group_width), bf16),
            pltpu.VMEM((2, tiles, all_rows, TILE), f32),
            pltpu.VMEM((tiles, all_rows, TILE), f32),
            pltpu.VMEM((all_rows, hidden), bf16),
            pltpu.VMEM((CHUNKS, 2, lines, rows, chunk), f32),
            pltpu.VMEM((CHUNKS, lines, rows, chunk), bf16),
            pltpu.VMEM((CHUNKS, lines, rows, chunk), bf16),
            pltpu.VMEM((CHUNKS, lines, rows, chunk), bf16),
            pltpu.VMEM((CHUNKS, lines, rows, chunk), bf16),
            dma((2,)),
            dma((5, groups)),
            dma((2, groups, lines)),
            dma((2, groups, lines)),
            dma((2, 2, groups)),
            dma((2, 2, groups, lines)),
            dma((2, 1)),
            dma((2, 1, lines)),
            dma((2, 1, lines)),
            dma((2, groups, lines)),
            dma((2, groups, lines)),
            dma((2, tiles)),
            dma((2, 1)),
            dma((2, CHUNKS)),
            dma((2, CHUNKS, lines)),
        ],
        compiler_params=pltpu.CompilerParams(
            collective_id=0, has_side_effects=True, vmem_limit_bytes=62 * 1024 * 1024
        ),
    )(
        queries,
        fresh_keys,
        fresh_values,
        residual_in,
        row_lengths,
        key_scales,
        value_scales,
        page_table,
        norm_gain.reshape(groups, 1, group_width),
        cache_keys,
        cache_values,
        w_gate,
        w_up,
        w_down,
    )


def choose_body(seq_size, cores, *args):
    local_rows, steps, width = args[0].shape
    groups, _, head_dim = args[4].shape
    rows, hidden = local_rows * steps, args[11].shape[1]
    stack = rows * width // (groups * head_dim)
    weights = 2 * 3 * width * hidden
    fits = (
        cores == 2
        and seq_size % 2 == 0
        and rows % 16 == 0
        and stack == 128
        and head_dim == 128
        and hidden % 256 == 0
        and hidden % (16 * groups) == 0
        and width % (16 * groups) == 0
        and width % (CHUNKS * TILE) == 0
        and CHUNKS % groups == 0
        and weights <= 44 * 1024 * 1024
    )
    if fits:
        return kernel_body(seq_size // 2, *args)
    return plain_body(*args)


def solution(mesh):
    in_specs = (
        P(("groups", "seq"), None, "tensor"),
        P(("groups", "seq"), None, "tensor"),
        P(("groups", "seq"), None, "tensor"),
        P(("groups", "seq"), None, "tensor"),
        P("tensor", ("groups", "seq"), None),
        P("tensor", ("groups", "seq"), None),
        P("tensor", ("groups", "seq")),
        P("tensor", ("groups", "seq")),
        P(("groups", "seq"), None),
        P("groups"),
        P("tensor"),
        P("tensor", "seq"),
        P("tensor", "seq"),
        P("seq", "tensor"),
    )
    out_specs = P(("groups", "seq"), None, "tensor")
    body = functools.partial(choose_body, mesh.shape["seq"], mesh.shape["tensor"])
    return jax.shard_map(body, mesh=mesh, in_specs=in_specs, out_specs=out_specs, check_vma=False)
```
